32 devices in a mesh: dp: 4 (over z), expert: 8 (over y, x, core).
Axes of the slice: x: 2, y: 2, z: 4, core: 2. Of those that a mesh axis runs over, the one named last changes fastest.
Arguments:
- tokens: bfloat16 [4096, 2048], P(('dp', 'expert')), may hold values from -6 to 6
- routes: int32 [4096, 8], P(('dp', 'expert')), may hold values from 0 to 15, all different within a row; in each aligned block of 128 rows (0 to 127, 128 to 255, ...) at most 96 rows name the same one
- route_weights: float32 [4096, 8], P(('dp', 'expert')), may hold values from 0.05 to 0.3
- cotangent: bfloat16 [4096, 2048], P(('dp', 'expert')), may hold values from -6 to 6
- gate_proj: bfloat16 [16, 2048, 640], P('expert'), may hold values from -0.125 to 0.125
- up_proj: bfloat16 [16, 2048, 640], P('expert'), may hold values from -0.125 to 0.125
- down_proj: bfloat16 [16, 640, 2048], P('expert'), may hold values from -0.25 to 0.25
Outputs:
- layer_output: bfloat16 [4096, 2048], P(('dp', 'expert'))
- input_grad: bfloat16 [4096, 2048], P(('dp', 'expert'))
- route_weight_grad: float32 [4096, 8], P(('dp', 'expert'))
- gate_grad: float32 [2048, 16, 640], P('dp', 'expert')
- up_grad: float32 [2048, 16, 640], P('dp', 'expert')
- down_grad: float32 [2048, 16, 640], P('dp', 'expert')
The draws below stay inside these ranges and needn't reach their ends.
Inputs may be any that keep to these rules, and one draw needn't show every extreme that they name: `routes`: each row names 8 different experts. Among the 128 rows of one device, no expert is named by more than 96 rows, a bound that some block reaches.
All inputs are finite; a program needn't handle non-finite values.
Results may differ from the reference program's by a relative error of at most 0.0095.
Values may be sent and summed in bfloat16 or wider, within the bound.
No kernel may reach another device: no remote copies, remote signals or barrier semaphores. Data moves between devices by JAX's collectives and lax.ppermute only.
A program may use at most 192 MiB of HBM per device.

```python
import math
import jax
import jax.numpy as jnp
import numpy as np
from jax import lax

D = 2048
HID = 640
TOP = 8
TOK_DEV = 128
EXPERTS = 16
CAP = 96
TOKENS = 4096
N_DP = 4
N_EXPERT = 8


def block_levels(key, dims, pieces, low, high):
    loudness, own = 1.0, jax.random.fold_in(key, 6)
    for dim, shards_of in pieces:
        steps = jnp.exp(jax.random.uniform(jax.random.fold_in(own, dim), (shards_of,), jnp.float32, low / len(pieces), high / len(pieces)))
        loudness = loudness * jnp.repeat(steps, dims[dim] // shards_of).reshape([-1 if axis == dim else 1 for axis in range(len(dims))])
    return loudness


def shared_out(own_key, own, number, rows, count, top, bound, lean):
    ranking = jax.random.permutation(own_key, count)
    crowded, common = load_shares(count, rows * top, bound, lean, True), load_shares(count, rows * top, bound, lean, False)
    places = jnp.arange(count)

    def named(sizes, rotation):
        used = int((sizes > 0).sum())
        fixed = max(1, used // 4)
        passed = fixed + (places - fixed + rotation * (used - fixed)) % max(1, count - fixed)
        return jnp.zeros((count,), jnp.int32).at[ranking[jnp.where(places < fixed, places, passed)]].set(jnp.asarray(sizes, jnp.int32))

    sizes = jnp.where(number % 4 == 0, named(crowded, number // 4), named(common, number - number // 4 - 1))
    mixed = jax.random.permutation(jax.random.fold_in(own, 3), count)
    giver, sink = mixed[0:count // 2 * 2:2], mixed[1:count // 2 * 2:2]
    room = jnp.minimum(sizes[giver] - 1, bound - sizes[sink]) // 2
    room = jnp.where((giver == ranking[0]) | (sink == ranking[0]) | (sizes[sink] == 0), 0, jnp.maximum(room, 0))
    passed = jax.random.randint(jax.random.fold_in(own, 4), (count // 2,), 0, 1 << 20) % (room + 1)
    sizes = sizes.at[giver].add(-passed).at[sink].add(passed)
    labels = jnp.searchsorted(jnp.cumsum(sizes), jnp.arange(rows * top), side="right").astype(jnp.int32)
    grid = labels.reshape(top, rows).T
    grid = grid[jax.random.permutation(jax.random.fold_in(own, 1), rows)]
    rotation = jax.random.randint(jax.random.fold_in(own, 2), (rows, 1), 0, top)
    return jnp.take_along_axis(grid, (jnp.arange(top)[None, :] + rotation) % top, axis=1)


def load_shares(count, total, limit, lean, full):
    loads = [(1 << 20) // math.isqrt(grade ** lean) + 1 for grade in range(1, count + 1)]
    largest = limit if full else min(limit, max(-(-total // count), total * loads[0] // sum(loads)))
    least = 1 if total - largest >= count - 1 else 0
    given, surplus = [largest] + [least] * (count - 1), total - largest - least * (count - 1)
    while surplus > 0:
        free = [i for i in range(1, count) if given[i] < largest] or [i for i in range(1, count) if given[i] < limit]
        pool, budget = sum([loads[i] for i in free]), surplus
        for i in free:
            extra = min(limit - given[i], max(1, budget * loads[i] // pool), surplus)
            given[i] = given[i] + extra
            surplus = surplus - extra
    return np.array(given)


def gaussian(own_key, shape, scale, bound, split=(), kind=jnp.bfloat16):
    values = scale * jax.random.normal(own_key, shape, jnp.float32)
    if split:
        values = values * block_levels(own_key, shape, split, -0.22, 0.18)
    return jnp.clip(values, -bound, bound).astype(kind)


def setup_inputs(seed: int = 0) -> dict:
    splits = jax.random.split(jax.random.key(seed), 8)
    tokens = gaussian(splits[0], (TOKENS, D), 1.0, 6.0, ((0, 32),))
    routes_keys = jax.random.split(jax.random.fold_in(splits[1], 1), TOKENS // TOK_DEV)
    routes_turns = jax.random.permutation(jax.random.fold_in(splits[1], 3), TOKENS // TOK_DEV)
    routes = jax.vmap(lambda own, number: shared_out(jax.random.fold_in(splits[1], 2), own, number, TOK_DEV, EXPERTS, TOP, CAP, 2))(routes_keys, routes_turns).reshape((TOKENS, TOP))
    route_weights = jnp.clip(0.05 + 0.25 * jax.random.uniform(splits[2], (TOKENS, TOP), jnp.float32) ** block_levels(splits[2], (TOKENS, TOP), ((0, 32),), -0.2, 0.2), 0.05, 0.3)
    cotangent = gaussian(splits[3], (TOKENS, D), 1.0, 6.0, ((0, 32),))
    gate_proj = gaussian(splits[4], (EXPERTS, D, HID), D ** -0.5, 0.125, ((0, 8),))
    up_proj = gaussian(splits[5], (EXPERTS, D, HID), D ** -0.5, 0.125, ((0, 8),))
    down_proj = gaussian(splits[6], (EXPERTS, HID, D), HID ** -0.5, 0.25, ((0, 8),))
    return dict(tokens=tokens, routes=routes, route_weights=route_weights, cotangent=cotangent, gate_proj=gate_proj, up_proj=up_proj, down_proj=down_proj)


def swish_parts(gate_pre):
    sig_value = jax.nn.sigmoid(gate_pre)
    return gate_pre * sig_value, sig_value * (1.0 + gate_pre * (1.0 - sig_value))


def reference(tokens, routes, route_weights, cotangent, gate_proj, up_proj, down_proj):
    n_tokens = tokens.shape[0]
    n_routes = n_tokens * TOP
    row_count = N_DP * N_EXPERT * CAP
    flat_expert = routes.reshape(-1).astype(jnp.int32)
    sort_order = jnp.argsort(flat_expert, stable=True).astype(jnp.int32)
    sorted_expert = flat_expert[sort_order]
    counts = jnp.zeros((EXPERTS,), jnp.int32).at[flat_expert].add(1)
    starts = (jnp.cumsum(counts) - counts).astype(jnp.int32)
    position = (jnp.arange(n_routes, dtype=jnp.int32) - starts[sorted_expert]).astype(jnp.int32)
    row_table = jnp.full((EXPERTS, row_count), n_routes, jnp.int32).at[sorted_expert, position].set(sort_order)
    tok_pad = jnp.concatenate([tokens, jnp.zeros((1, D), tokens.dtype)], 0)
    cot_pad = jnp.concatenate([cotangent, jnp.zeros((1, D), cotangent.dtype)], 0)
    weight_pad = jnp.concatenate([route_weights.reshape(-1), jnp.zeros((1,), jnp.float32)], 0)

    def one_expert(state_now, per_expert):
        out_acc, grad_acc, weight_acc = state_now
        row_index, gate_mat, up_mat, down_mat = per_expert
        token_row = (row_index // TOP).astype(jnp.int32)
        rows_in = tok_pad[token_row]
        rows_cot = cot_pad[token_row]
        row_weight = weight_pad[row_index]
        gate_pre = jnp.dot(rows_in, gate_mat, preferred_element_type=jnp.float32)
        up_pre = jnp.dot(rows_in, up_mat, preferred_element_type=jnp.float32)
        swish, d_swish = swish_parts(gate_pre)
        hidden = (swish * up_pre).astype(jnp.bfloat16)
        route_out = jnp.dot(hidden, down_mat, preferred_element_type=jnp.float32).astype(jnp.bfloat16)
        out_acc = out_acc.at[token_row].add(row_weight[:, None] * route_out.astype(jnp.float32))
        weight_grad = jnp.sum(route_out.astype(jnp.float32) * rows_cot.astype(jnp.float32), axis=1)
        weight_acc = weight_acc.at[row_index].set(weight_grad)
        route_cot = (row_weight[:, None] * rows_cot.astype(jnp.float32)).astype(jnp.bfloat16)
        d_hidden = jnp.dot(route_cot, down_mat.T, preferred_element_type=jnp.float32)
        d_gate = (d_hidden * up_pre * d_swish).astype(jnp.bfloat16)
        d_up = (d_hidden * swish).astype(jnp.bfloat16)
        route_dx = (jnp.dot(d_gate, gate_mat.T, preferred_element_type=jnp.float32)
                    + jnp.dot(d_up, up_mat.T, preferred_element_type=jnp.float32)).astype(jnp.bfloat16)
        grad_acc = grad_acc.at[token_row].add(route_dx.astype(jnp.float32))
        gate_g = jnp.dot(rows_in.T, d_gate, preferred_element_type=jnp.float32)
        up_g = jnp.dot(rows_in.T, d_up, preferred_element_type=jnp.float32)
        down_g = jnp.dot(route_cot.T, hidden, preferred_element_type=jnp.float32)
        return (out_acc, grad_acc, weight_acc), (gate_g, up_g, down_g)

    start_state = (jnp.zeros((n_tokens + 1, D), jnp.float32), jnp.zeros((n_tokens + 1, D), jnp.float32),
                   jnp.zeros((n_routes + 1,), jnp.float32))
    final_state, grads = lax.scan(one_expert, start_state, (row_table, gate_proj, up_proj, down_proj))
    out_acc, grad_acc, weight_acc = final_state
    layer_output = out_acc[:n_tokens].astype(jnp.bfloat16)
    input_grad = grad_acc[:n_tokens].astype(jnp.bfloat16)
    route_weight_grad = weight_acc[:n_routes].reshape(n_tokens, TOP)
    gate_grad = jnp.transpose(grads[0], (1, 0, 2))
    up_grad = jnp.transpose(grads[1], (1, 0, 2))
    down_grad = jnp.transpose(grads[2], (1, 0, 2))
    return (layer_output, input_grad, route_weight_grad, gate_grad, up_grad, down_grad)
```

```python
import functools

import jax
import jax.numpy as jnp
from jax import lax
from jax.experimental import pallas as pl
from jax.experimental.pallas import tpu as pltpu
from jax.sharding import PartitionSpec as P

VMEM_BYTES = 56 * 1024 * 1024


def swap(value, axis, mask):
    return lax.ppermute(value, axis, [(i, i ^ mask) for i in range(lax.axis_size(axis))])


def way_bits(axis):
    bits = [1 << b for b in range(1, lax.axis_size(axis).bit_length() - 1)]
    return list(zip(bits, bits[::-1]))


def gather_rows(own, axis):
    half = own.shape[0] // 2
    first, second = own[:half], own[half:]
    for bit_first, bit_second in way_bits(axis):
        first, second = (
            jnp.concatenate([first, swap(first, axis, bit_first)], 0),
            jnp.concatenate([second, swap(second, axis, bit_second)], 0),
        )
    both = jnp.concatenate([first, second], 0)
    return jnp.concatenate([both, swap(both, axis, 1)], 0)


def add_to(kept, received):
    return (kept.astype(jnp.float32) + received.astype(jnp.float32)).astype(kept.dtype)


def scatter_rows(parts, axis):
    half = parts.shape[0] // 2
    both = add_to(parts[:half], swap(parts[half:], axis, 1))
    half = half // 2
    first, second = both[:half], both[half:]
    for bit_first, bit_second in way_bits(axis)[::-1]:
        half = half // 2
        first, second = (
            add_to(first[:half], swap(first[half:], axis, bit_first)),
            add_to(second[:half], swap(second[half:], axis, bit_second)),
        )
    return jnp.concatenate([first, second], 0)


def routes_kernel(hid, x_ref, c_ref, w_ref, wgu_ref, wd_ref, hw_ref, dgu_ref, rwg_ref):
    cols = wd_ref.shape[0]
    x, c = x_ref[...], c_ref[...]
    weight = w_ref[...]
    step = 256 if cols % 256 == 0 else 128
    sums = [jnp.zeros((x.shape[0], 1), jnp.float32) for _ in range(cols // hid)]
    for start in range(0, cols, step):
        gate = jnp.dot(x, wgu_ref[:, start : start + step], preferred_element_type=jnp.float32)
        up = jnp.dot(
            x, wgu_ref[:, cols + start : cols + start + step], preferred_element_type=jnp.float32
        )
        d_plain = lax.dot_general(
            c,
            wd_ref[start : start + step, :],
            (((1,), (1,)), ((), ())),
            preferred_element_type=jnp.float32,
        )
        sig = jax.nn.sigmoid(gate)
        swish = gate * sig
        d_swish = sig * (1.0 + gate * (1.0 - sig))
        hidden = swish * up
        product = hidden * d_plain
        for lane in range(0, step, 128):
            here = slice(lane, lane + 128)
            e = (start + lane) // hid
            w = weight[:, e : e + 1]
            d_hidden = d_plain[:, here] * w
            at = start + lane
            hw_ref[:, at : at + 128] = (hidden[:, here] * w).astype(jnp.bfloat16)
            dgu_ref[:, at : at + 128] = (d_hidden * up[:, here] * d_swish[:, here]).astype(
                jnp.bfloat16
            )
            dgu_ref[:, cols + at : cols + at + 128] = (d_hidden * swish[:, here]).astype(
                jnp.bfloat16
            )
            sums[e] = sums[e] + jnp.sum(product[:, here], axis=1, keepdims=True)
    rwg_ref[...] = jnp.concatenate(sums, axis=1)


def routes_pass(x, c, weight, wgu, wd, hid):
    rows, width = x.shape
    cols = wd.shape[0]
    tile = min(256, rows)
    return pl.pallas_call(
        functools.partial(routes_kernel, hid),
        grid=(rows // tile,),
        in_specs=[
            pl.BlockSpec((tile, width), lambda i: (i, 0)),
            pl.BlockSpec((tile, width), lambda i: (i, 0)),
            pl.BlockSpec((tile, weight.shape[1]), lambda i: (i, 0)),
            pl.BlockSpec(wgu.shape, lambda i: (0, 0), pipeline_mode=pl.Buffered(1)),
            pl.BlockSpec(wd.shape, lambda i: (0, 0), pipeline_mode=pl.Buffered(1)),
        ],
        out_specs=[
            pl.BlockSpec((tile, cols), lambda i: (i, 0)),
            pl.BlockSpec((tile, 2 * cols), lambda i: (i, 0)),
            pl.BlockSpec((tile, weight.shape[1]), lambda i: (i, 0)),
        ],
        out_shape=[
            jax.ShapeDtypeStruct((rows, cols), jnp.bfloat16),
            jax.ShapeDtypeStruct((rows, 2 * cols), jnp.bfloat16),
            jax.ShapeDtypeStruct((rows, weight.shape[1]), jnp.float32),
        ],
        compiler_params=pltpu.CompilerParams(vmem_limit_bytes=VMEM_BYTES),
        cost_estimate=pl.CostEstimate(
            flops=6 * rows * width * cols,
            bytes_accessed=2 * (2 * rows * width + 3 * width * cols + 3 * rows * cols),
            transcendentals=rows * cols,
        ),
        name="routes_pass",
    )(x, c, weight, wgu, wd)


def halving_plan(masks):
    keep = [0]
    for mask in masks[1:]:
        keep = keep + [mask ^ k for k in keep]
    return keep, [masks[0] ^ k for k in keep]


def slots_of(order, wanted):
    slots, writes, last = [], [], wanted.index(next(r for r in order if r in wanted))
    for rel in order:
        if rel in wanted:
            last = wanted.index(rel)
        slots.append(last)
        writes.append(int(rel in wanted))
    return slots, writes


def grad_kernel(block_ref, slot_ref, write_ref, src_ref, rhs_ref, *outs):
    j = pl.program_id(0)
    hid = outs[0].shape[-1]
    value = lax.dot_general(
        src_ref[...], rhs_ref[...], (((0,), (0,)), ((), ())), preferred_element_type=jnp.float32
    ).astype(jnp.bfloat16)
    for n, out in enumerate(outs):

        @pl.when(write_ref[n, j] == 1)
        def _(out=out, e=n // 2):
            out[...] = value[None, :, e * hid : (e + 1) * hid]


def grad_pass(src, rhs, part, experts, n_dp, masks, relative):
    rows, width = src.shape
    own = width // n_dp
    cols = rhs.shape[1] // part[1]
    hid = cols // experts
    plans = [halving_plan(masks if e % 2 == 0 else masks[::-1]) for e in range(experts)]
    order = [r for r in range(1, n_dp)] + [0]
    slots, writes = [], []
    for keep, send in plans:
        for wanted in (keep, send):
            s, w = slots_of(order, wanted)
            slots.append(s)
            writes.append(w)
    blocks = relative[jnp.array(order, jnp.int32)]
    specs = [
        pl.BlockSpec((1, own, hid), functools.partial(lambda n, j, b, s, w: (s[n, j], 0, 0), n))
        for n in range(2 * experts)
    ]
    outs = pl.pallas_call(
        grad_kernel,
        grid_spec=pltpu.PrefetchScalarGridSpec(
            num_scalar_prefetch=3,
            grid=(n_dp,),
            in_specs=[
                pl.BlockSpec((rows, own), lambda j, b, s, w: (0, b[j])),
                pl.BlockSpec(
                    (rows, cols), lambda j, b, s, w: (0, part[0]), pipeline_mode=pl.Buffered(1)
                ),
            ],
            out_specs=specs,
        ),
        out_shape=[jax.ShapeDtypeStruct((n_dp // 2, own, hid), jnp.bfloat16)] * (2 * experts),
        compiler_params=pltpu.CompilerParams(vmem_limit_bytes=VMEM_BYTES),
        cost_estimate=pl.CostEstimate(
            flops=2 * rows * width * cols,
            bytes_accessed=2 * (rows * width + rows * cols + width * cols),
            transcendentals=0,
        ),
        name="grad_pass",
    )(blocks, jnp.array(slots, jnp.int32), jnp.array(writes, jnp.int32), src, rhs)
    return [(outs[2 * e], outs[2 * e + 1]) for e in range(experts)]


def reduce_blocks(keep, send, masks, axis):
    for n, mask in enumerate(masks):
        got = swap(send, axis, mask)
        if n == len(masks) - 1:
            return keep[0].astype(jnp.float32) + got[0].astype(jnp.float32)
        total = add_to(keep, got)
        half = total.shape[0] // 2
        keep, send = total[:half], total[half:]


def on_device(tokens, routes, route_weights, cotangent, gate_proj, up_proj, down_proj):
    width = tokens.shape[1]
    exp_dev, hid = down_proj.shape[:2]
    groups = lax.axis_size("expert")
    n_dp = lax.axis_size("dp")
    experts = exp_dev * groups
    mine = lax.axis_index("expert") * exp_dev
    masks = [(2 << b) - 1 for b in range(n_dp.bit_length() - 1)]
    relative = lax.axis_index("dp") ^ jnp.arange(n_dp, dtype=jnp.int32)

    named = routes[:, :, None] == jnp.arange(experts, dtype=jnp.int32)[None, None, :]
    dense = jnp.sum(jnp.where(named, route_weights[:, :, None], 0.0), axis=1)
    x = gather_rows(tokens, "expert")
    c = gather_rows(cotangent, "expert")
    weight = lax.dynamic_slice_in_dim(gather_rows(dense, "expert"), mine, exp_dev, 1)

    wgu = jnp.concatenate([gate_proj[e] for e in range(exp_dev)] + [up_proj[e] for e in range(exp_dev)], 1)
    wd = down_proj.reshape(exp_dev * hid, width)
    hw, dgu, rwg = routes_pass(x, c, weight, wgu, wd, hid)

    gate_parts = grad_pass(x, dgu, (0, 2), exp_dev, n_dp, masks, relative)
    up_parts = grad_pass(x, dgu, (1, 2), exp_dev, n_dp, masks, relative)
    down_parts = grad_pass(c, hw, (0, 1), exp_dev, n_dp, masks, relative)
    grads = [
        jnp.stack(
            [
                reduce_blocks(keep, send, masks if e % 2 == 0 else masks[::-1], "dp")
                for e, (keep, send) in enumerate(parts)
            ],
            axis=1,
        )
        for parts in (gate_parts, up_parts, down_parts)
    ]

    out = jnp.dot(hw, wd, preferred_element_type=jnp.float32).astype(jnp.bfloat16)
    dx = lax.dot_general(
        dgu, wgu, (((1,), (1,)), ((), ())), preferred_element_type=jnp.float32
    ).astype(jnp.bfloat16)
    layer_output = scatter_rows(out, "expert")
    input_grad = scatter_rows(dx, "expert")
    spread = lax.dynamic_update_slice_in_dim(
        jnp.zeros((rwg.shape[0], experts), jnp.float32), rwg, mine, 1
    )
    rwg_dense = scatter_rows(spread, "expert")
    route_weight_grad = jnp.sum(jnp.where(named, rwg_dense[:, None, :], 0.0), axis=2)
    return (layer_output, input_grad, route_weight_grad, *grads)


def solution(mesh):
    rows = P(("dp", "expert"), None)
    held = P("expert", None, None)
    owned = P("dp", "expert", None)
    return jax.shard_map(
        on_device,
        mesh=mesh,
        in_specs=(rows, rows, rows, rows, held, held, held),
        out_specs=(rows, rows, rows, owned, owned, owned),
        check_vma=False,
    )
```

```python
import functools

import jax
import jax.numpy as jnp
from jax import lax
from jax.experimental import pallas as pl
from jax.experimental.pallas import tpu as pltpu
from jax.sharding import PartitionSpec as P

MIB = 1024 * 1024
DECLARED = 1 << 20
ROUTES_BYTES, OUT_BYTES, GRAD_BYTES, SUM_BYTES = 56 * MIB, 56 * MIB, 56 * MIB, 8 * MIB


def swap(value, axis, mask):
    return lax.ppermute(value, axis, [(i, i ^ mask) for i in range(lax.axis_size(axis))])


def together(values):
    return list(lax.optimization_barrier(tuple(values)))


def way_bits(axis):
    bits = [1 << b for b in range(1, lax.axis_size(axis).bit_length() - 1)]
    return list(zip(bits, bits[::-1]))


def join(parts):
    return parts[0] if len(parts) == 1 else jnp.concatenate(parts, 0)


def gather_planes(own, masks, work):
    pieces, halves, made, tied = [], own, [], 0
    ways = way_bits("expert")
    for n in range(len(masks)):
        first, second = halves
        for s, (bit_first, bit_second) in enumerate(ways):
            sent = [swap(first, "expert", bit_first), swap(second, "expert", bit_second)]
            if s == len(ways) - 1 and n + 1 < len(masks):
                sent += [swap(half, "dp", masks[n + 1]) for half in own]
            beside = []
            if pieces:
                pieces[-1].append(swap(pieces[-1][0], "expert", 1))
                made.append(work(pieces[-1], len(pieces) <= len(ways)))
            ended = range(tied, len(made) if len(sent) > 2 else len(made) - 1)
            for p in ended:
                beside += made[p]
            got = together(sent + beside)
            rest = got[len(sent) :]
            for p in ended:
                made[p], rest = rest[: len(made[p])], rest[len(made[p]) :]
                tied = p + 1
            halves = got[2 : len(sent)]
            whole = [join([first, got[0]]), join([second, got[1]])]
            pieces.append([join(whole if s == 0 else got[:2])])
            first, second = whole
    pieces[-1].append(swap(pieces[-1][0], "expert", 1))
    made.append(work(pieces[-1], len(pieces) <= len(ways)))
    return pieces, made


def add_to(kept, received):
    return (kept.astype(jnp.float32) + received.astype(jnp.float32)).astype(kept.dtype)


def scatter_round(sides, s, bits, beside):
    if s == 0:
        sides = [[p[0][: p[0].shape[0] // 2], p[0][p[0].shape[0] // 2 :]] for p in sides]
    *beside, first, second = together(
        beside + [swap(side[-1], "expert", bit) for side, bit in zip(sides, bits)]
    )
    summed = []
    for side, value in zip(sides, (first, second)):
        at, kept = 0, []
        for part in side[:-1]:
            kept.append(add_to(part, value[at : at + part.shape[0]]))
            at += part.shape[0]
        summed.append(kept)
    return summed, beside


def tile_of(cols):
    return 256 if cols % 256 == 0 else 128


def split_in_two(value):
    high = value.astype(jnp.bfloat16)
    return high, (value - high.astype(jnp.float32)).astype(jnp.bfloat16)


def by_expert(values, lane, hid):
    spread = values[-1]
    for e in range(len(values) - 2, -1, -1):
        spread = jnp.where(lane < (e + 1) * hid, values[e], spread)
    return spread


def routes_kernel(blocks, hid, experts, with_rwg, mine_ref, *refs):
    xcs, (wg, wu, wd, hw, dg, du, *more) = refs[:blocks], refs[blocks:]
    extra_ref, sums = more[0] if with_rwg else None, more[-1]
    j, (tile, width) = pl.program_id(0), wd.shape
    held = sums.shape[1]

    @pl.when(j == 0)
    def _():
        sums[...] = jnp.zeros(sums.shape, jnp.float32)

    mine = mine_ref[0]
    end = 0
    for xc in xcs:
        rows = slice(end, end + xc.shape[0])
        end = rows.stop
        lane = lax.broadcasted_iota(jnp.int32, (xc.shape[0], tile), 1) + j * tile
        tail = xc[:, 2 * width :].astype(jnp.float32)
        spot = lax.broadcasted_iota(jnp.int32, tail.shape, 1)
        spots = [(spot == mine + e, spot == experts + mine + e) for e in range(held)]
        weights = [
            jnp.sum(jnp.where(high | low, tail, 0.0), axis=1, keepdims=True) for high, low in spots
        ]
        gate = jnp.dot(xc[:, :width], wg[...], preferred_element_type=jnp.float32)
        up = jnp.dot(xc[:, :width], wu[...], preferred_element_type=jnp.float32)
        d_plain = lax.dot_general(
            xc[:, width : 2 * width],
            wd[...],
            (((1,), (1,)), ((), ())),
            preferred_element_type=jnp.float32,
        )
        weight = by_expert(weights, lane, hid)
        sig = jax.nn.sigmoid(gate)
        swish = gate * sig
        hidden = swish * up
        d_hidden = d_plain * weight
        hw[rows, :] = (hidden * weight).astype(jnp.bfloat16)
        dg[rows, :] = (d_hidden * up * (sig * (1.0 + gate * (1.0 - sig)))).astype(jnp.bfloat16)
        du[rows, :] = (d_hidden * swish).astype(jnp.bfloat16)
        if not with_rwg:
            continue
        product = hidden * d_plain
        for e in range(held):
            inside = (lane >= e * hid) & (lane < (e + 1) * hid)
            sums[rows, e : e + 1] += jnp.sum(
                jnp.where(inside, product, 0.0), axis=1, keepdims=True
            )

    if with_rwg:

        @pl.when(j == pl.num_programs(0) - 1)
        def _():
            spot = lax.broadcasted_iota(jnp.int32, extra_ref.shape, 1)
            placed = jnp.zeros(extra_ref.shape, jnp.float32)
            for e in range(held):
                top, rest = split_in_two(sums[:, e : e + 1])
                placed = jnp.where(spot == mine + e, top.astype(jnp.float32), placed)
                placed = jnp.where(spot == experts + mine + e, rest.astype(jnp.float32), placed)
            extra_ref[...] = placed.astype(jnp.bfloat16)


def routes_pass(blocks, mine, wgu, wd, hid, experts, with_rwg):
    rows, wide = sum(block.shape[0] for block in blocks), blocks[0].shape[1]
    cols, width = wd.shape
    tile, once = tile_of(cols), pl.Buffered(1)
    steps = cols // tile
    extra = wide - 2 * width
    return pl.pallas_call(
        functools.partial(routes_kernel, len(blocks), hid, experts, with_rwg),
        grid=(steps,),
        in_specs=[pl.BlockSpec(memory_space=pltpu.SMEM)]
        + [pl.BlockSpec(b.shape, lambda j: (0, 0), pipeline_mode=once) for b in blocks]
        + [
            pl.BlockSpec((width, tile), lambda j: (0, j)),
            pl.BlockSpec((width, tile), lambda j: (0, steps + j)),
            pl.BlockSpec((tile, width), lambda j: (j, 0)),
        ],
        out_specs=[pl.BlockSpec((rows, tile), lambda j: (0, j))] * 3
        + [pl.BlockSpec((rows, extra), lambda j: (0, 0))] * with_rwg,
        out_shape=[jax.ShapeDtypeStruct((rows, cols), jnp.bfloat16)] * 3
        + [jax.ShapeDtypeStruct((rows, extra), jnp.bfloat16)] * with_rwg,
        scratch_shapes=[pltpu.VMEM((rows, cols // hid), jnp.float32)],
        compiler_params=pltpu.CompilerParams(vmem_limit_bytes=ROUTES_BYTES),
        cost_estimate=pl.CostEstimate(
            flops=6 * rows * width * cols // DECLARED,
            bytes_accessed=2 * (2 * rows * width + 3 * width * cols) // DECLARED,
            transcendentals=0,
        ),
        name="routes_pass",
    )(mine, *blocks, wgu, wgu, wd)


def out_kernel(pieces, token_ref, *refs):
    made, (wd, wgu), outs = refs[: 4 * pieces], refs[4 * pieces : 4 * pieces + 2], refs[4 * pieces + 2 :]
    j, steps = pl.program_id(0), (pl.num_programs(0) - 1) // 2
    tile = wd.shape[1]
    cols = wd.shape[0]

    def put(p, value):
        half = value.shape[0] // 2
        outs[2 * p][:, : value.shape[1]] = value[:half].astype(jnp.bfloat16)
        outs[2 * p + 1][:, : value.shape[1]] = value[half:].astype(jnp.bfloat16)

    for p in range(pieces):
        hw, dg, du, extra = made[4 * p : 4 * p + 4]

        @pl.when(j < steps)
        def _():
            put(p, jnp.dot(hw[...], wd[...], preferred_element_type=jnp.float32))

        @pl.when((j >= steps) & (j < 2 * steps))
        def _():
            put(
                p,
                sum(
                    lax.dot_general(
                        d[...],
                        wgu[:, at : at + cols],
                        (((1,), (1,)), ((), ())),
                        preferred_element_type=jnp.float32,
                    )
                    for d, at in ((dg, 0), (du, cols))
                ),
            )

        @pl.when(j == 2 * steps)
        def _():
            put(p, extra[...])


def out_pass(made, wgu, wd, token):
    cols, width = wd.shape
    tile = 512 if width % 512 == 0 else 128
    steps, wide = width // tile, 2 * width + made[0][3].shape[1]
    flat = [value for each in made for value in each]
    outs = []
    for each in made:
        outs += [jax.ShapeDtypeStruct((each[0].shape[0] // 2, wide), jnp.bfloat16)] * 2
    rows = sum(each[0].shape[0] for each in made)
    got = pl.pallas_call(
        functools.partial(out_kernel, len(made)),
        grid=(2 * steps + 1,),
        in_specs=[pl.BlockSpec(memory_space=pltpu.SMEM)]
        + [pl.BlockSpec(v.shape, lambda j: (0, 0), pipeline_mode=pl.Buffered(1)) for v in flat]
        + [
            pl.BlockSpec((cols, tile), lambda j: (0, jnp.minimum(j, steps - 1))),
            pl.BlockSpec((tile, 2 * cols), lambda j: (jnp.clip(j - steps, 0, steps - 1), 0)),
        ],
        out_specs=[pl.BlockSpec((o.shape[0], tile), lambda j: (0, j)) for o in outs],
        out_shape=outs,
        compiler_params=pltpu.CompilerParams(vmem_limit_bytes=OUT_BYTES),
        cost_estimate=pl.CostEstimate(
            flops=(6 * rows * width * cols) // DECLARED,
            bytes_accessed=2 * (2 * rows * width + 3 * width * cols) // DECLARED,
            transcendentals=0,
        ),
        name="out_pass",
    )(token, *flat, wd, wgu)
    return list(got)


def grad_kernel(sources, parts, block_ref, *refs):
    srcs, rhss, refs = refs[:sources], refs[sources : sources + parts], refs[sources + parts :]
    j, out_ref, turned = pl.program_id(0), refs[-2], refs[-1]

    @pl.when(j == 0)
    def _():
        at = 0
        for src in srcs:
            turned[:, at : at + src.shape[0]] = src[...].T
            at += src.shape[0]

    rhs = jnp.concatenate([ref[...] for ref in rhss], 0)
    total = jnp.dot(turned[...], rhs, preferred_element_type=jnp.float32)
    if len(refs) == 2:
        out_ref[...] = total.astype(out_ref.dtype)
    else:
        total = total + refs[0][...].astype(jnp.float32)
        for e in range(out_ref.shape[1]):

            @pl.when(j == e)
            def _():
                out_ref[:, e, :] = total


def grad_pass(srcs, rhss, block, own, hid, name, first=0, exp_dev=None, got=None):
    rows, cols = sum(src.shape[0] for src in srcs), exp_dev * hid
    in_specs = [pl.BlockSpec((src.shape[0], own), lambda j, b: (0, b[0])) for src in srcs]
    in_specs += [pl.BlockSpec((rhs.shape[0], hid), lambda j, b: (0, first + j)) for rhs in rhss]
    out_spec = pl.BlockSpec((own, hid), lambda j, b: (0, j))
    out_shape = jax.ShapeDtypeStruct((own, cols), jnp.bfloat16)
    operands = [*srcs, *rhss]
    if got is not None:
        in_specs.append(out_spec)
        operands.append(got)
        out_spec = pl.BlockSpec((own, exp_dev, hid), lambda j, b: (0, 0, 0))
        out_shape = jax.ShapeDtypeStruct((own, exp_dev, hid), jnp.float32)
    return pl.pallas_call(
        functools.partial(grad_kernel, len(srcs), len(rhss)),
        grid_spec=pltpu.PrefetchScalarGridSpec(
            num_scalar_prefetch=1,
            grid=(exp_dev,),
            in_specs=in_specs,
            out_specs=out_spec,
            scratch_shapes=[pltpu.VMEM((own, rows), jnp.bfloat16)],
        ),
        out_shape=out_shape,
        compiler_params=pltpu.CompilerParams(vmem_limit_bytes=GRAD_BYTES),
        cost_estimate=pl.CostEstimate(
            flops=2 * rows * own * cols // DECLARED,
            bytes_accessed=2 * (rows * (own + cols) + own * cols) // DECLARED,
            transcendentals=0,
        ),
        name=name,
    )(block, *operands)


def sum_kernel(keep_ref, got_ref, out_ref):
    total = keep_ref[...].astype(jnp.float32) + got_ref[...].astype(jnp.float32)
    hid = out_ref.shape[2]
    for e in range(out_ref.shape[1]):
        out_ref[:, e, :] = total[:, e * hid : (e + 1) * hid]


def sum_pass(keep, got, exp_dev):
    rows, cols = keep.shape
    tile = min(128, rows)
    block = pl.BlockSpec((tile, cols), lambda i: (i, 0))
    return pl.pallas_call(
        sum_kernel,
        grid=(rows // tile,),
        in_specs=[block, block],
        out_specs=pl.BlockSpec((tile, exp_dev, cols // exp_dev), lambda i: (i, 0, 0)),
        out_shape=jax.ShapeDtypeStruct((rows, exp_dev, cols // exp_dev), jnp.float32),
        compiler_params=pltpu.CompilerParams(vmem_limit_bytes=SUM_BYTES),
        name="sum_pass",
    )(keep, got)


def dense_form(tokens, routes, route_weights, cotangent, gate_proj, up_proj, down_proj):
    tok_dev, width = tokens.shape
    exp_dev, hid = down_proj.shape[:2]
    cols = exp_dev * hid
    n_dp = lax.axis_size("dp")
    own = width // n_dp
    experts = exp_dev * lax.axis_size("expert")
    mine = (lax.axis_index("expert") * exp_dev).reshape(1).astype(jnp.int32)
    here = lax.axis_index("dp")

    named = routes[:, :, None] == jnp.arange(experts, dtype=jnp.int32)[None, None, :]
    dense = jnp.sum(jnp.where(named, route_weights[:, :, None], 0.0), axis=1)
    high = lax.reduce_precision(dense, 8, 7)
    space = -(2 * experts) % 128
    xc = jnp.concatenate(
        [tokens, cotangent, high.astype(jnp.bfloat16), (dense - high).astype(jnp.bfloat16)]
        + [jnp.zeros((tok_dev, space), jnp.bfloat16)],
        1,
    )
    wgu = jnp.concatenate(
        [gate_proj[e] for e in range(exp_dev)] + [up_proj[e] for e in range(exp_dev)], 1
    )
    wd = down_proj.reshape(cols, width)

    def work(blocks, with_rwg):
        return list(routes_pass(blocks, mine, wgu, wd, hid, experts, with_rwg))

    halves = [xc[: tok_dev // 2], xc[tok_dev // 2 :]]
    pieces, made = gather_planes(halves, list(range(0, n_dp, 2)), work)
    arrived = [block for piece in pieces for block in piece]
    hws, dgs, dus = [[values[n] for values in made] for n in range(3)]
    own_made = made[: len(way_bits("expert"))]
    mates, token = (here ^ 1).reshape(1).astype(jnp.int32), here.reshape(1).astype(jnp.int32)

    def grad(rhss, block, of_cot, name, first=0, count=exp_dev, got=None):
        block = block + (n_dp if of_cot else 0)
        return grad_pass(arrived, rhss, block, own, hid, name, first, count, got)

    gate_send, mates = together([grad(dgs, mates, False, "gate_send"), mates])
    up_send, after = together([grad(dus, mates, False, "up_send"), mates])
    gate_got, up_send, mates, token, *shares = together(
        [swap(gate_send, "dp", 1), up_send, after, token] + out_pass(own_made, wgu, wd, after)
    )
    chip = [add_to(k, swap(v, "expert", 1)) for k, v in zip(shares[::2], shares[1::2])]
    down_send = grad(hws, mates, True, "down_send")
    *chip[-1:], token, down_send = together([chip[-1], token, down_send])
    sides = [[p[: p.shape[0] // 2] for p in chip], [p[p.shape[0] // 2 :] for p in chip]]
    gate_grad = grad(dgs, token, False, "gate_grad", got=gate_got)
    beside = [swap(up_send, "dp", 1), down_send, gate_grad, token]
    rounds = list(enumerate(way_bits("expert")))[::-1]
    for s, bits in rounds[:-1]:
        sides, beside = scatter_round(sides, s, bits, beside)
    up_got, down_send, gate_grad, token = beside
    down_got = swap(down_send, "dp", 1)
    up_grad = grad(dus, token, False, "up_grad", got=up_got)
    down_keep = grad(hws, token, True, "down_keep")
    sides, (down_got, up_grad, down_keep) = scatter_round(
        sides, *rounds[-1], [down_got, up_grad, down_keep]
    )
    summed = join([sides[0][0], sides[1][0]])
    grads = [gate_grad, up_grad, sum_pass(down_keep, down_got, exp_dev)]

    tail = summed[:, 2 * width :].astype(jnp.float32)
    rwg_dense = tail[:, :experts] + tail[:, experts : 2 * experts]
    route_weight_grad = jnp.sum(jnp.where(named, rwg_dense[:, None, :], 0.0), axis=2)
    return (summed[:, :width], summed[:, width : 2 * width], route_weight_grad, *grads)


def swish_parts(gate_pre):
    sig_value = jax.nn.sigmoid(gate_pre)
    return (gate_pre * sig_value, sig_value * (1.0 + gate_pre * (1.0 - sig_value)))


def project_in(arrived, gate_proj, up_proj):
    gate_pre = jnp.einsum("secd,edh->sech", arrived, gate_proj, preferred_element_type=jnp.float32)
    up_pre = jnp.einsum("secd,edh->sech", arrived, up_proj, preferred_element_type=jnp.float32)
    return (gate_pre, up_pre)


def project_out(gate_pre, up_pre, down_proj):
    swish = swish_parts(gate_pre)[0]
    hidden = (swish * up_pre).astype(jnp.bfloat16)
    return jnp.einsum(
        "sech,ehd->secd", hidden, down_proj, preferred_element_type=jnp.float32
    ).astype(jnp.bfloat16)


def three_terms(feat_rows, cot_rows, d_gate, d_up, hidden):
    return jnp.stack(
        [
            jnp.einsum("secd,sech->deh", feat_rows, d_gate, preferred_element_type=jnp.float32),
            jnp.einsum("secd,sech->deh", feat_rows, d_up, preferred_element_type=jnp.float32),
            jnp.einsum("secd,sech->deh", cot_rows, hidden, preferred_element_type=jnp.float32),
        ],
        axis=1,
    )


def slots_form(tokens, routes, route_weights, cotangent, gate_proj, up_proj, down_proj):
    tok_dev, model_width = tokens.shape
    top_count = routes.shape[1]
    exp_dev = gate_proj.shape[0]
    groups = lax.axis_size("expert")
    experts = exp_dev * groups
    capacity = 3 * tok_dev * top_count // (2 * experts)
    n_routes = tok_dev * top_count
    flat_expert = routes.reshape(-1)
    onehot = (flat_expert[:, None] == jnp.arange(experts, dtype=jnp.int32)[None, :]).astype(
        jnp.int32
    )
    before = jnp.cumsum(onehot, axis=0) - onehot
    position = jnp.sum(before * onehot, axis=1)
    slot_index = flat_expert * capacity + position
    slot_source = (
        jnp.full((experts * capacity,), n_routes, jnp.int32)
        .at[slot_index]
        .set(jnp.arange(n_routes, dtype=jnp.int32))
    )
    token_of = slot_source // top_count
    padded_x = jnp.concatenate([tokens, jnp.zeros((1, model_width), tokens.dtype)], 0)
    outgoing = padded_x[token_of].reshape(groups, exp_dev, capacity, model_width)
    arrived = lax.all_to_all(outgoing, "expert", split_axis=0, concat_axis=0, tiled=True)
    gate_pre, up_pre = project_in(arrived, gate_proj, up_proj)
    expert_out, arrived, gate_pre, up_pre = (
        project_out(gate_pre, up_pre, down_proj),
        arrived,
        gate_pre,
        up_pre,
    )
    returned = lax.all_to_all(expert_out, "expert", split_axis=0, concat_axis=0, tiled=True)
    route_out = returned.reshape(experts * capacity, model_width)[slot_index].reshape(
        tok_dev, top_count, model_width
    )
    layer_output = jnp.sum(
        route_out.astype(jnp.float32) * route_weights[:, :, None], axis=1
    ).astype(jnp.bfloat16)
    route_weight_grad = jnp.einsum(
        "tkd,td->tk", route_out, cotangent, preferred_element_type=jnp.float32
    )
    route_cot = (route_weights[:, :, None] * cotangent[:, None, :].astype(jnp.float32)).astype(
        jnp.bfloat16
    )
    padded_cot = jnp.concatenate(
        [route_cot.reshape(n_routes, model_width), jnp.zeros((1, model_width), jnp.bfloat16)], 0
    )
    cot_out = padded_cot[slot_source].reshape(groups, exp_dev, capacity, model_width)
    arrived_cot = lax.all_to_all(cot_out, "expert", split_axis=0, concat_axis=0, tiled=True)
    swish, d_swish = swish_parts(gate_pre)
    hidden = (swish * up_pre).astype(jnp.bfloat16)
    d_hidden = jnp.einsum(
        "secd,ehd->sech", arrived_cot, down_proj, preferred_element_type=jnp.float32
    )
    d_gate = (d_hidden * up_pre * d_swish).astype(jnp.bfloat16)
    d_up = (d_hidden * swish).astype(jnp.bfloat16)
    route_dx = (
        jnp.einsum("sech,edh->secd", d_gate, gate_proj, preferred_element_type=jnp.float32)
        + jnp.einsum("sech,edh->secd", d_up, up_proj, preferred_element_type=jnp.float32)
    ).astype(jnp.bfloat16)
    dx_back = lax.all_to_all(route_dx, "expert", split_axis=0, concat_axis=0, tiled=True)
    token_dx = dx_back.reshape(experts * capacity, model_width)[slot_index].reshape(
        tok_dev, top_count, model_width
    )
    input_grad = jnp.sum(token_dx.astype(jnp.float32), axis=1).astype(jnp.bfloat16)
    full_terms = three_terms(arrived, arrived_cot, d_gate, d_up, hidden)
    shares = lax.psum_scatter(
        full_terms.astype(jnp.bfloat16), "dp", scatter_dimension=0, tiled=True
    ).astype(jnp.float32)
    return (layer_output, input_grad, route_weight_grad, shares[:, 0], shares[:, 1], shares[:, 2])


def on_device(tokens, routes, route_weights, cotangent, gate_proj, up_proj, down_proj):
    experts = gate_proj.shape[0] * lax.axis_size("expert")
    form = dense_form if experts <= 2 * routes.shape[1] else slots_form
    return form(tokens, routes, route_weights, cotangent, gate_proj, up_proj, down_proj)


def solution(mesh):
    rows = P(("dp", "expert"), None)
    held = P("expert", None, None)
    owned = P("dp", "expert", None)
    return jax.shard_map(
        on_device,
        mesh=mesh,
        in_specs=(rows, rows, rows, rows, held, held, held),
        out_specs=(rows, rows, rows, owned, owned, owned),
        check_vma=False,
    )
```

```python
import functools

import jax
import jax.numpy as jnp
from jax import lax
from jax.experimental import pallas as pl
from jax.experimental.pallas import tpu as pltpu
from jax.sharding import PartitionSpec as P

MIB = 1024 * 1024
DECLARED = 1 << 20
ROUTES_BYTES, OUT_BYTES, GRAD_BYTES, SUM_BYTES = 56 * MIB, 56 * MIB, 56 * MIB, 8 * MIB


def swap(value, axis, mask):
    return lax.ppermute(value, axis, [(i, i ^ mask) for i in range(lax.axis_size(axis))])


def together(values):
    return list(lax.optimization_barrier(tuple(values)))


def join(parts):
    return parts[0] if len(parts) == 1 else jnp.concatenate(parts, 0)


def add_to(kept, received):
    return (kept.astype(jnp.float32) + received.astype(jnp.float32)).astype(kept.dtype)


def tile_of(cols):
    return 256 if cols % 256 == 0 else 128


def split_in_two(value):
    high = value.astype(jnp.bfloat16)
    return high, (value - high.astype(jnp.float32)).astype(jnp.bfloat16)


def by_expert(values, lane, hid):
    spread = values[-1]
    for e in range(len(values) - 2, -1, -1):
        spread = jnp.where(lane < (e + 1) * hid, values[e], spread)
    return spread


def routes_kernel(counts, hid, experts, with_rwg, mine_ref, *refs):
    xcs, (wg, wu, wd, hw, dg, du, *more) = refs[: sum(counts)], refs[sum(counts) :]
    extra_ref, sums = more[0] if with_rwg else None, more[-1]
    j, (tile, width) = pl.program_id(0), wd.shape
    held = sums.shape[1]

    @pl.when(j == 0)
    def _():
        sums[...] = jnp.zeros(sums.shape, jnp.float32)

    mine = mine_ref[0]
    end = 0
    for count in counts:
        group, xcs = xcs[:count], xcs[count:]
        x = jnp.concatenate([ref[:, :width] for ref in group], 0)
        c = jnp.concatenate([ref[:, width : 2 * width] for ref in group], 0)
        tail = jnp.concatenate([ref[:, 2 * width :] for ref in group], 0).astype(jnp.float32)
        rows = slice(end, end + x.shape[0])
        end = rows.stop
        lane = lax.broadcasted_iota(jnp.int32, (x.shape[0], tile), 1) + j * tile
        spot = lax.broadcasted_iota(jnp.int32, tail.shape, 1)
        spots = [(spot == mine + e, spot == experts + mine + e) for e in range(held)]
        weights = [
            jnp.sum(jnp.where(high | low, tail, 0.0), axis=1, keepdims=True) for high, low in spots
        ]
        gate = jnp.dot(x, wg[...], preferred_element_type=jnp.float32)
        up = jnp.dot(x, wu[...], preferred_element_type=jnp.float32)
        d_plain = lax.dot_general(
            c,
            wd[...],
            (((1,), (1,)), ((), ())),
            preferred_element_type=jnp.float32,
        )
        weight = by_expert(weights, lane, hid)
        sig = jax.nn.sigmoid(gate)
        swish = gate * sig
        hidden = swish * up
        d_hidden = d_plain * weight
        hw[rows, :] = (hidden * weight).astype(jnp.bfloat16)
        dg[rows, :] = (d_hidden * up * (sig * (1.0 + gate * (1.0 - sig)))).astype(jnp.bfloat16)
        du[rows, :] = (d_hidden * swish).astype(jnp.bfloat16)
        if not with_rwg:
            continue
        product = hidden * d_plain
        for e in range(held):
            inside = (lane >= e * hid) & (lane < (e + 1) * hid)
            sums[rows, e : e + 1] += jnp.sum(
                jnp.where(inside, product, 0.0), axis=1, keepdims=True
            )

    if with_rwg:

        @pl.when(j == pl.num_programs(0) - 1)
        def _():
            spot = lax.broadcasted_iota(jnp.int32, extra_ref.shape, 1)
            placed = jnp.zeros(extra_ref.shape, jnp.float32)
            for e in range(held):
                top, rest = split_in_two(sums[:, e : e + 1])
                placed = jnp.where(spot == mine + e, top.astype(jnp.float32), placed)
                placed = jnp.where(spot == experts + mine + e, rest.astype(jnp.float32), placed)
            extra_ref[...] = placed.astype(jnp.bfloat16)


def routes_pass(groups, mine, wgu, wd, hid, experts, with_rwg, declared=DECLARED):
    counts, blocks = [len(group) for group in groups], [b for group in groups for b in group]
    rows, wide = sum(block.shape[0] for block in blocks), blocks[0].shape[1]
    cols, width = wd.shape
    tile, once = tile_of(cols), pl.Buffered(1)
    steps = cols // tile
    extra = wide - 2 * width
    return pl.pallas_call(
        functools.partial(routes_kernel, counts, hid, experts, with_rwg),
        grid=(steps,),
        in_specs=[pl.BlockSpec(memory_space=pltpu.SMEM)]
        + [pl.BlockSpec(b.shape, lambda j: (0, 0), pipeline_mode=once) for b in blocks]
        + [
            pl.BlockSpec((width, tile), lambda j: (0, j)),
            pl.BlockSpec((width, tile), lambda j: (0, steps + j)),
            pl.BlockSpec((tile, width), lambda j: (j, 0)),
        ],
        out_specs=[pl.BlockSpec((rows, tile), lambda j: (0, j))] * 3
        + [pl.BlockSpec((rows, extra), lambda j: (0, 0))] * with_rwg,
        out_shape=[jax.ShapeDtypeStruct((rows, cols), jnp.bfloat16)] * 3
        + [jax.ShapeDtypeStruct((rows, extra), jnp.bfloat16)] * with_rwg,
        scratch_shapes=[pltpu.VMEM((rows, cols // hid), jnp.float32)],
        compiler_params=pltpu.CompilerParams(vmem_limit_bytes=ROUTES_BYTES),
        cost_estimate=pl.CostEstimate(
            flops=6 * rows * width * cols // declared,
            bytes_accessed=2 * (2 * rows * width + 3 * width * cols) // declared,
            transcendentals=0,
        ),
        name="routes_pass",
    )(mine, *blocks, wgu, wgu, wd)


def out_kernel(sections, token_ref, *refs):
    made, (wd, wgu), outs = refs[: 4 * sections], refs[4 * sections : 4 * sections + 2], refs[4 * sections + 2 :]
    j, steps = pl.program_id(0), (pl.num_programs(0) - 1) // 2
    cols = wd.shape[0]

    def put(p, value):
        half, tile = value.shape[0] // 2, value.shape[1]
        outs[2 * p][:, :tile] = value[:half].astype(jnp.bfloat16)
        outs[2 * p + 1][:, :tile] = value[half:].astype(jnp.bfloat16)

    for p in range(sections):
        hw, dg, du, extra = made[4 * p : 4 * p + 4]

        @pl.when(j < steps)
        def _():
            put(p, jnp.dot(hw[...], wd[...], preferred_element_type=jnp.float32))

        @pl.when((j >= steps) & (j < 2 * steps))
        def _():
            put(
                p,
                sum(
                    lax.dot_general(
                        d[...],
                        wgu[:, at : at + cols],
                        (((1,), (1,)), ((), ())),
                        preferred_element_type=jnp.float32,
                    )
                    for d, at in ((dg, 0), (du, cols))
                ),
            )

        @pl.when(j == 2 * steps)
        def _():
            put(p, extra[...])


def out_pass(sections, wgu, wd, token):
    cols, width = wd.shape
    tile = 512 if width % 512 == 0 else 128
    steps, wide = width // tile, 2 * width + sections[0][0][3].shape[1]
    flat, specs, outs = [], [], []
    for values, rows in sections:
        flat += values
        specs += [
            pl.BlockSpec((rows, v.shape[1]), lambda j: (0, 0), pipeline_mode=pl.Buffered(1))
            for v in values
        ]
        outs += [jax.ShapeDtypeStruct((rows // 2, wide), jnp.bfloat16)] * 2
    total = sum(rows for _, rows in sections)
    got = pl.pallas_call(
        functools.partial(out_kernel, len(sections)),
        grid=(2 * steps + 1,),
        in_specs=[pl.BlockSpec(memory_space=pltpu.SMEM)]
        + specs
        + [
            pl.BlockSpec((cols, tile), lambda j: (0, jnp.minimum(j, steps - 1))),
            pl.BlockSpec((tile, 2 * cols), lambda j: (jnp.clip(j - steps, 0, steps - 1), 0)),
        ],
        out_specs=[pl.BlockSpec((o.shape[0], tile), lambda j: (0, j)) for o in outs],
        out_shape=outs,
        compiler_params=pltpu.CompilerParams(vmem_limit_bytes=OUT_BYTES),
        cost_estimate=pl.CostEstimate(
            flops=6 * total * width * cols // DECLARED,
            bytes_accessed=2 * (2 * total * width + 3 * width * cols) // DECLARED,
            transcendentals=0,
        ),
        name="out_pass",
    )(token, *flat, wd, wgu)
    return list(got)


def grad_kernel(sources, sets, parts, exp_dev, given, block_ref, *refs):
    srcs, refs = refs[:sources], refs[sources:]
    rhss, refs = [refs[t * parts : (t + 1) * parts] for t in range(sets)], refs[sets * parts :]
    j, gots, outs, turned = pl.program_id(0), refs[:given], refs[given:-1], refs[-1]

    @pl.when(j == 0)
    def _():
        at = 0
        for src in srcs:
            turned[:, at : at + src.shape[0]] = src[...].T
            at += src.shape[0]

    for t in range(sets):

        @pl.when((j >= t * exp_dev) & (j < (t + 1) * exp_dev))
        def _():
            rhs = jnp.concatenate([ref[...] for ref in rhss[t]], 0)
            total = jnp.dot(turned[...], rhs, preferred_element_type=jnp.float32)
            if not gots:
                if len(outs) == 1:
                    outs[0][...] = total.astype(jnp.bfloat16)
                for n, out in enumerate(outs if len(outs) > 1 else []):

                    @pl.when(j == n)
                    def _():
                        out[...] = total.astype(jnp.bfloat16)

                return
            for e in range(exp_dev):

                @pl.when(j == t * exp_dev + e)
                def _():
                    outs[t][:, e, :] = total + gots[e % given][...].astype(jnp.float32)


def grad_pass(srcs, sets, block, own, exp_dev, name, got=(), apart=False):
    rows, hid = sum(src.shape[0] for src in srcs), sets[0][0].shape[1] // exp_dev
    cols = len(sets) * exp_dev * hid
    in_specs = [pl.BlockSpec((src.shape[0], own), lambda j, b: (0, b[0])) for src in srcs]
    for t, rhss in enumerate(sets):
        in_specs += [
            pl.BlockSpec(
                (rhs.shape[0], hid),
                functools.partial(
                    lambda first, j, b: (0, jnp.clip(j - first, 0, exp_dev - 1)), t * exp_dev
                ),
            )
            for rhs in rhss
        ]
    out_specs = [pl.BlockSpec((own, hid), lambda j, b: (0, j))]
    out_shape = [jax.ShapeDtypeStruct((own, cols), jnp.bfloat16)]
    operands = [*srcs, *(rhs for rhss in sets for rhs in rhss)]
    if apart:
        out_specs = [pl.BlockSpec((own, hid), lambda j, b: (0, 0))] * (cols // hid)
        out_shape = [jax.ShapeDtypeStruct((own, hid), jnp.bfloat16)] * (cols // hid)
    if got:
        apart_spec = pl.BlockSpec((own, hid), lambda j, b: (0, 0))
        in_specs += out_specs if len(got) == 1 else [apart_spec] * len(got)
        operands += got
        out_specs = [pl.BlockSpec((own, exp_dev, hid), lambda j, b: (0, 0, 0))] * len(sets)
        out_shape = [jax.ShapeDtypeStruct((own, exp_dev, hid), jnp.float32)] * len(sets)
    return pl.pallas_call(
        functools.partial(grad_kernel, len(srcs), len(sets), len(sets[0]), exp_dev, len(got)),
        grid_spec=pltpu.PrefetchScalarGridSpec(
            num_scalar_prefetch=1,
            grid=(len(sets) * exp_dev,),
            in_specs=in_specs,
            out_specs=out_specs,
            scratch_shapes=[pltpu.VMEM((own, rows), jnp.bfloat16)],
        ),
        out_shape=out_shape,
        compiler_params=pltpu.CompilerParams(vmem_limit_bytes=GRAD_BYTES),
        cost_estimate=pl.CostEstimate(
            flops=2 * rows * own * cols // DECLARED,
            bytes_accessed=2 * (rows * (own + cols) + own * cols) // DECLARED,
            transcendentals=0,
        ),
        name=name,
    )(block, *operands)


def sum_kernel(keep_ref, *refs):
    gots, out_ref = refs[:-1], refs[-1]
    hid = out_ref.shape[2]
    for e, got_ref in enumerate(gots):
        keep = keep_ref[:, e * hid : (e + 1) * hid].astype(jnp.float32)
        out_ref[:, e, :] = keep + got_ref[...].astype(jnp.float32)


def sum_pass(keep, gots):
    rows, cols = keep.shape
    tile, hid = min(128, rows), cols // len(gots)
    return pl.pallas_call(
        sum_kernel,
        grid=(rows // tile,),
        in_specs=[pl.BlockSpec((tile, cols), lambda i: (i, 0))]
        + [pl.BlockSpec((tile, hid), lambda i: (i, 0))] * len(gots),
        out_specs=pl.BlockSpec((tile, len(gots), hid), lambda i: (i, 0, 0)),
        out_shape=jax.ShapeDtypeStruct((rows, len(gots), hid), jnp.float32),
        compiler_params=pltpu.CompilerParams(vmem_limit_bytes=SUM_BYTES),
        name="sum_pass",
    )(keep, *gots)


def dense_form(tokens, routes, route_weights, cotangent, gate_proj, up_proj, down_proj):
    tok_dev, width = tokens.shape
    exp_dev, hid = down_proj.shape[:2]
    cols = exp_dev * hid
    n_dp = lax.axis_size("dp")
    own = width // n_dp
    experts = exp_dev * lax.axis_size("expert")
    mine = (lax.axis_index("expert") * exp_dev).reshape(1).astype(jnp.int32)
    here = lax.axis_index("dp")

    named = routes[:, :, None] == jnp.arange(experts, dtype=jnp.int32)[None, None, :]
    dense = jnp.sum(jnp.where(named, route_weights[:, :, None], 0.0), axis=1)
    high = lax.reduce_precision(dense, 8, 7)
    space = -(2 * experts) % 128
    xc = jnp.concatenate(
        [tokens, cotangent, high.astype(jnp.bfloat16), (dense - high).astype(jnp.bfloat16)]
        + [jnp.zeros((tok_dev, space), jnp.bfloat16)],
        1,
    )
    wgu = jnp.concatenate(
        [gate_proj[e] for e in range(exp_dev)] + [up_proj[e] for e in range(exp_dev)], 1
    )
    wd = down_proj.reshape(cols, width)

    def work(groups, with_rwg, **kwargs):
        return list(routes_pass(groups, mine, wgu, wd, hid, experts, with_rwg, **kwargs))

    def across(*blocks):
        return [swap(block, "expert", 1) for block in blocks]

    half = tok_dev // 2
    by_x, by_y = 2, 4
    mate = swap(xc, "dp", 2)
    near_x, near_y = together([swap(xc, "expert", by_x), swap(xc, "expert", by_y)])
    near = [xc, near_x, near_y]
    first = near + across(*near)
    corner = [swap(near_x[:half], "expert", by_y), swap(near_y[half:], "expert", by_x)]
    made = work([first[:2], first[2:4], first[4:]], True)
    corner_x, corner_y, mate, *first_made = together([*corner, mate, *made])
    corner = [corner_x, corner_y]
    second = corner + across(*corner) + [mate] + across(mate)
    made = work([second[:4], second[4:]], True)
    far_x, far_y, *second_made = together(
        [swap(mate, "expert", by_x), swap(mate, "expert", by_y), *made]
    )
    third = [far_x, far_y] + across(far_x, far_y)
    corner = [swap(far_x[:half], "expert", by_y), swap(far_y[half:], "expert", by_x)]
    made = work([third[:2], third[2:]], False)
    corner_x, corner_y, *third_made = together([*corner, *made])
    fourth = [corner_x, corner_y] + across(corner_x, corner_y)
    fourth_made = work([fourth], False)
    arrived = first + second + third + fourth
    units = [first_made, second_made, third_made, fourth_made]
    hws, dgs, dus = [[values[n] for values in units] for n in range(3)]
    mates, token = (here ^ 1).reshape(1).astype(jnp.int32), here.reshape(1).astype(jnp.int32)

    def grad(sets, block, of_cot, name, got=(), apart=False):
        block = block + (n_dp if of_cot else 0)
        return grad_pass(arrived, sets, block, own, exp_dev, name, got, apart)

    gate_send, mates = together([*grad([dgs], mates, False, "gate_send"), mates])
    *up_send, after = together([*grad([dus], mates, False, "up_send", apart=True), mates])
    shares = out_pass([(first_made, 6 * tok_dev), (second_made, 2 * tok_dev)], wgu, wd, after)
    *shares, mates = together([*shares, after])
    down_send = grad([hws], mates, True, "down_send", apart=True)
    *values, up_last, gate_got, token = together(
        [*shares, *down_send, *(swap(send, "dp", 1) for send in up_send[:-1])]
        + [up_send[-1], swap(gate_send, "dp", 1), token]
    )
    shares, down_send, up_got = values[:4], values[4 : 4 + exp_dev], values[4 + exp_dev :]
    corner = add_to(shares[2], *across(shares[3]))
    chip = add_to(shares[0], *across(shares[1]))
    corner, token = together([corner, token])
    (down_keep,) = grad([hws], token, True, "down_keep")
    to_x, to_y, up_last, chip, down_keep, token, *down_send = together(
        [
            swap(corner[:half], "expert", by_y),
            swap(corner[half:], "expert", by_x),
            swap(up_last, "dp", 1),
            chip,
            down_keep,
            token,
            *down_send,
        ]
    )
    *down_got, last_got = [swap(send, "dp", 1) for send in down_send]
    mine_too, of_x, of_y = chip[:tok_dev], chip[tok_dev : 2 * tok_dev], chip[2 * tok_dev :]
    of_x = join([add_to(of_x[:half], to_x), of_x[half:]])
    of_y = join([of_y[:half], add_to(of_y[half:], to_y)])
    (gate_grad,) = grad([dgs], token, False, "gate_grad", got=[gate_got])
    (up_grad,) = grad([dus], token, False, "up_grad", got=[*up_got, up_last])
    from_x, from_y, gate_grad, up_grad, *down_got = together(
        [swap(of_x, "expert", by_x), swap(of_y, "expert", by_y), gate_grad, up_grad, *down_got]
    )
    summed = sum(v.astype(jnp.float32) for v in (mine_too, from_x, from_y))
    tail = summed[:, 2 * width :]
    rwg_dense = tail[:, :experts] + tail[:, experts : 2 * experts]
    route_weight_grad = jnp.sum(jnp.where(named, rwg_dense[:, None, :], 0.0), axis=2)
    summed = summed[:, : 2 * width].astype(jnp.bfloat16)
    layer_output, input_grad, route_weight_grad, last_got = together(
        [summed[:, :width], summed[:, width:], route_weight_grad, last_got]
    )
    grads = [gate_grad, up_grad, sum_pass(down_keep, [*down_got, last_got])]
    return (layer_output, input_grad, route_weight_grad, *grads)


def swish_parts(gate_pre):
    sig_value = jax.nn.sigmoid(gate_pre)
    return (gate_pre * sig_value, sig_value * (1.0 + gate_pre * (1.0 - sig_value)))


def project_in(arrived, gate_proj, up_proj):
    gate_pre = jnp.einsum("secd,edh->sech", arrived, gate_proj, preferred_element_type=jnp.float32)
    up_pre = jnp.einsum("secd,edh->sech", arrived, up_proj, preferred_element_type=jnp.float32)
    return (gate_pre, up_pre)


def project_out(gate_pre, up_pre, down_proj):
    swish = swish_parts(gate_pre)[0]
    hidden = (swish * up_pre).astype(jnp.bfloat16)
    return jnp.einsum(
        "sech,ehd->secd", hidden, down_proj, preferred_element_type=jnp.float32
    ).astype(jnp.bfloat16)


def three_terms(feat_rows, cot_rows, d_gate, d_up, hidden):
    return jnp.stack(
        [
            jnp.einsum("secd,sech->deh", feat_rows, d_gate, preferred_element_type=jnp.float32),
            jnp.einsum("secd,sech->deh", feat_rows, d_up, preferred_element_type=jnp.float32),
            jnp.einsum("secd,sech->deh", cot_rows, hidden, preferred_element_type=jnp.float32),
        ],
        axis=1,
    )


def slots_form(tokens, routes, route_weights, cotangent, gate_proj, up_proj, down_proj):
    tok_dev, model_width = tokens.shape
    top_count = routes.shape[1]
    exp_dev = gate_proj.shape[0]
    groups = lax.axis_size("expert")
    experts = exp_dev * groups
    capacity = 3 * tok_dev * top_count // (2 * experts)
    n_routes = tok_dev * top_count
    flat_expert = routes.reshape(-1)
    onehot = (flat_expert[:, None] == jnp.arange(experts, dtype=jnp.int32)[None, :]).astype(
        jnp.int32
    )
    before = jnp.cumsum(onehot, axis=0) - onehot
    position = jnp.sum(before * onehot, axis=1)
    slot_index = flat_expert * capacity + position
    slot_source = (
        jnp.full((experts * capacity,), n_routes, jnp.int32)
        .at[slot_index]
        .set(jnp.arange(n_routes, dtype=jnp.int32))
    )
    token_of = slot_source // top_count
    padded_x = jnp.concatenate([tokens, jnp.zeros((1, model_width), tokens.dtype)], 0)
    outgoing = padded_x[token_of].reshape(groups, exp_dev, capacity, model_width)
    arrived = lax.all_to_all(outgoing, "expert", split_axis=0, concat_axis=0, tiled=True)
    gate_pre, up_pre = project_in(arrived, gate_proj, up_proj)
    expert_out, arrived, gate_pre, up_pre = (
        project_out(gate_pre, up_pre, down_proj),
        arrived,
        gate_pre,
        up_pre,
    )
    returned = lax.all_to_all(expert_out, "expert", split_axis=0, concat_axis=0, tiled=True)
    route_out = returned.reshape(experts * capacity, model_width)[slot_index].reshape(
        tok_dev, top_count, model_width
    )
    layer_output = jnp.sum(
        route_out.astype(jnp.float32) * route_weights[:, :, None], axis=1
    ).astype(jnp.bfloat16)
    route_weight_grad = jnp.einsum(
        "tkd,td->tk", route_out, cotangent, preferred_element_type=jnp.float32
    )
    route_cot = (route_weights[:, :, None] * cotangent[:, None, :].astype(jnp.float32)).astype(
        jnp.bfloat16
    )
    padded_cot = jnp.concatenate(
        [route_cot.reshape(n_routes, model_width), jnp.zeros((1, model_width), jnp.bfloat16)], 0
    )
    cot_out = padded_cot[slot_source].reshape(groups, exp_dev, capacity, model_width)
    arrived_cot = lax.all_to_all(cot_out, "expert", split_axis=0, concat_axis=0, tiled=True)
    swish, d_swish = swish_parts(gate_pre)
    hidden = (swish * up_pre).astype(jnp.bfloat16)
    d_hidden = jnp.einsum(
        "secd,ehd->sech", arrived_cot, down_proj, preferred_element_type=jnp.float32
    )
    d_gate = (d_hidden * up_pre * d_swish).astype(jnp.bfloat16)
    d_up = (d_hidden * swish).astype(jnp.bfloat16)
    route_dx = (
        jnp.einsum("sech,edh->secd", d_gate, gate_proj, preferred_element_type=jnp.float32)
        + jnp.einsum("sech,edh->secd", d_up, up_proj, preferred_element_type=jnp.float32)
    ).astype(jnp.bfloat16)
    dx_back = lax.all_to_all(route_dx, "expert", split_axis=0, concat_axis=0, tiled=True)
    token_dx = dx_back.reshape(experts * capacity, model_width)[slot_index].reshape(
        tok_dev, top_count, model_width
    )
    input_grad = jnp.sum(token_dx.astype(jnp.float32), axis=1).astype(jnp.bfloat16)
    full_terms = three_terms(arrived, arrived_cot, d_gate, d_up, hidden)
    shares = lax.psum_scatter(
        full_terms.astype(jnp.bfloat16), "dp", scatter_dimension=0, tiled=True
    ).astype(jnp.float32)
    return (layer_output, input_grad, route_weight_grad, shares[:, 0], shares[:, 1], shares[:, 2])


def on_device(tokens, routes, route_weights, cotangent, gate_proj, up_proj, down_proj):
    groups = lax.axis_size("expert")
    few = gate_proj.shape[0] * groups <= 2 * routes.shape[1]
    square = groups == 2 * 2 * 2 and lax.axis_size("dp") == 2 * 2
    form = dense_form if few and square else slots_form
    return form(tokens, routes, route_weights, cotangent, gate_proj, up_proj, down_proj)


def solution(mesh):
    rows = P(("dp", "expert"), None)
    held = P("expert", None, None)
    owned = P("dp", "expert", None)
    return jax.shard_map(
        on_device,
        mesh=mesh,
        in_specs=(rows, rows, rows, rows, held, held, held),
        out_specs=(rows, rows, rows, owned, owned, owned),
        check_vma=False,
    )
```

```python
import functools

import jax
import jax.numpy as jnp
from jax import lax
from jax.experimental import pallas as pl
from jax.experimental.pallas import tpu as pltpu
from jax.sharding import PartitionSpec as P

MIB = 1024 * 1024
DECLARED = 1 << 20
ROUTES_BYTES, OUT_BYTES, GRAD_BYTES, SUM_BYTES = 56 * MIB, 56 * MIB, 56 * MIB, 8 * MIB


def swap(value, axis, mask):
    return lax.ppermute(value, axis, [(i, i ^ mask) for i in range(lax.axis_size(axis))])


def together(values):
    return list(lax.optimization_barrier(tuple(values)))


def join(parts):
    return parts[0] if len(parts) == 1 else jnp.concatenate(parts, 0)


def add_to(kept, received):
    return (kept.astype(jnp.float32) + received.astype(jnp.float32)).astype(kept.dtype)


def tile_of(cols):
    return 256 if cols % 256 == 0 else 128


def split_in_two(value):
    high = value.astype(jnp.bfloat16)
    return high, (value - high.astype(jnp.float32)).astype(jnp.bfloat16)


def by_expert(values, lane, hid):
    spread = values[-1]
    for e in range(len(values) - 2, -1, -1):
        spread = jnp.where(lane < (e + 1) * hid, values[e], spread)
    return spread


def routes_kernel(counts, hid, experts, with_rwg, mine_ref, *refs):
    xcs, (wg, wu, wd, hw, dg, du, *more) = refs[: sum(counts)], refs[sum(counts) :]
    extra_ref, sums = more[0] if with_rwg else None, more[-1]
    j, (tile, width) = pl.program_id(0), wd.shape
    held = sums.shape[1]

    @pl.when(j == 0)
    def _():
        sums[...] = jnp.zeros(sums.shape, jnp.float32)

    mine = mine_ref[0]
    end = 0
    for count in counts:
        group, xcs = xcs[:count], xcs[count:]
        x = jnp.concatenate([ref[:, :width] for ref in group], 0)
        c = jnp.concatenate([ref[:, width : 2 * width] for ref in group], 0)
        tail = jnp.concatenate([ref[:, 2 * width :] for ref in group], 0).astype(jnp.float32)
        rows = slice(end, end + x.shape[0])
        end = rows.stop
        lane = lax.broadcasted_iota(jnp.int32, (x.shape[0], tile), 1) + j * tile
        spot = lax.broadcasted_iota(jnp.int32, tail.shape, 1)
        spots = [(spot == mine + e, spot == experts + mine + e) for e in range(held)]
        weights = [
            jnp.sum(jnp.where(high | low, tail, 0.0), axis=1, keepdims=True) for high, low in spots
        ]
        gate = jnp.dot(x, wg[...], preferred_element_type=jnp.float32)
        up = jnp.dot(x, wu[...], preferred_element_type=jnp.float32)
        d_plain = lax.dot_general(
            c,
            wd[...],
            (((1,), (1,)), ((), ())),
            preferred_element_type=jnp.float32,
        )
        weight = by_expert(weights, lane, hid)
        sig = jax.nn.sigmoid(gate)
        swish = gate * sig
        hidden = swish * up
        d_hidden = d_plain * weight
        hw[rows, :] = (hidden * weight).astype(jnp.bfloat16)
        dg[rows, :] = (d_hidden * up * (sig * (1.0 + gate * (1.0 - sig)))).astype(jnp.bfloat16)
        du[rows, :] = (d_hidden * swish).astype(jnp.bfloat16)
        if not with_rwg:
            continue
        product = hidden * d_plain
        for e in range(held):
            inside = (lane >= e * hid) & (lane < (e + 1) * hid)
            sums[rows, e : e + 1] += jnp.sum(
                jnp.where(inside, product, 0.0), axis=1, keepdims=True
            )

    if with_rwg:

        @pl.when(j == pl.num_programs(0) - 1)
        def _():
            spot = lax.broadcasted_iota(jnp.int32, extra_ref.shape, 1)
            placed = jnp.zeros(extra_ref.shape, jnp.float32)
            for e in range(held):
                top, rest = split_in_two(sums[:, e : e + 1])
                placed = jnp.where(spot == mine + e, top.astype(jnp.float32), placed)
                placed = jnp.where(spot == experts + mine + e, rest.astype(jnp.float32), placed)
            extra_ref[...] = placed.astype(jnp.bfloat16)


def routes_pass(groups, mine, wgu, wd, hid, experts, with_rwg, declared=DECLARED):
    counts, blocks = [len(group) for group in groups], [b for group in groups for b in group]
    rows, wide = sum(block.shape[0] for block in blocks), blocks[0].shape[1]
    cols, width = wd.shape
    tile, once = tile_of(cols), pl.Buffered(1)
    steps = cols // tile
    extra = wide - 2 * width
    return pl.pallas_call(
        functools.partial(routes_kernel, counts, hid, experts, with_rwg),
        grid=(steps,),
        in_specs=[pl.BlockSpec(memory_space=pltpu.SMEM)]
        + [pl.BlockSpec(b.shape, lambda j: (0, 0), pipeline_mode=once) for b in blocks]
        + [
            pl.BlockSpec((width, tile), lambda j: (0, j)),
            pl.BlockSpec((width, tile), lambda j: (0, steps + j)),
            pl.BlockSpec((tile, width), lambda j: (j, 0)),
        ],
        out_specs=[pl.BlockSpec((rows, tile), lambda j: (0, j))] * 3
        + [pl.BlockSpec((rows, extra), lambda j: (0, 0))] * with_rwg,
        out_shape=[jax.ShapeDtypeStruct((rows, cols), jnp.bfloat16)] * 3
        + [jax.ShapeDtypeStruct((rows, extra), jnp.bfloat16)] * with_rwg,
        scratch_shapes=[pltpu.VMEM((rows, cols // hid), jnp.float32)],
        compiler_params=pltpu.CompilerParams(vmem_limit_bytes=ROUTES_BYTES),
        cost_estimate=pl.CostEstimate(
            flops=6 * rows * width * cols // declared,
            bytes_accessed=2 * (2 * rows * width + 3 * width * cols) // declared,
            transcendentals=0,
        ),
        name="routes_pass",
    )(mine, *blocks, wgu, wgu, wd)


def out_kernel(sections, token_ref, *refs):
    made, (wd, wgu), outs = refs[: 4 * sections], refs[4 * sections : 4 * sections + 2], refs[4 * sections + 2 :]
    j, steps = pl.program_id(0), (pl.num_programs(0) - 1) // 2
    cols = wd.shape[0]

    def put(p, value):
        half, tile = value.shape[0] // 2, value.shape[1]
        outs[2 * p][:, :tile] = value[:half].astype(jnp.bfloat16)
        outs[2 * p + 1][:, :tile] = value[half:].astype(jnp.bfloat16)

    for p in range(sections):
        hw, dg, du, extra = made[4 * p : 4 * p + 4]

        @pl.when(j < steps)
        def _():
            put(p, jnp.dot(hw[...], wd[...], preferred_element_type=jnp.float32))

        @pl.when((j >= steps) & (j < 2 * steps))
        def _():
            put(
                p,
                sum(
                    lax.dot_general(
                        d[...],
                        wgu[:, at : at + cols],
                        (((1,), (1,)), ((), ())),
                        preferred_element_type=jnp.float32,
                    )
                    for d, at in ((dg, 0), (du, cols))
                ),
            )

        @pl.when(j == 2 * steps)
        def _():
            put(p, extra[...])


def out_pass(sections, wgu, wd, token):
    cols, width = wd.shape
    tile = 512 if width % 512 == 0 else 128
    steps, wide = width // tile, 2 * width + sections[0][0][3].shape[1]
    flat, specs, outs = [], [], []
    for values, rows in sections:
        flat += values
        specs += [
            pl.BlockSpec((rows, v.shape[1]), lambda j: (0, 0), pipeline_mode=pl.Buffered(1))
            for v in values
        ]
        outs += [jax.ShapeDtypeStruct((rows // 2, wide), jnp.bfloat16)] * 2
    total = sum(rows for _, rows in sections)
    got = pl.pallas_call(
        functools.partial(out_kernel, len(sections)),
        grid=(2 * steps + 1,),
        in_specs=[pl.BlockSpec(memory_space=pltpu.SMEM)]
        + specs
        + [
            pl.BlockSpec((cols, tile), lambda j: (0, jnp.minimum(j, steps - 1))),
            pl.BlockSpec((tile, 2 * cols), lambda j: (jnp.clip(j - steps, 0, steps - 1), 0)),
        ],
        out_specs=[pl.BlockSpec((o.shape[0], tile), lambda j: (0, j)) for o in outs],
        out_shape=outs,
        compiler_params=pltpu.CompilerParams(vmem_limit_bytes=OUT_BYTES),
        cost_estimate=pl.CostEstimate(
            flops=6 * total * width * cols // DECLARED,
            bytes_accessed=2 * (2 * total * width + 3 * width * cols) // DECLARED,
            transcendentals=0,
        ),
        name="out_pass",
    )(token, *flat, wd, wgu)
    return list(got)


def grad_kernel(sources, sets, parts, exp_dev, given, block_ref, *refs):
    srcs, refs = refs[:sources], refs[sources:]
    rhss, refs = [refs[t * parts : (t + 1) * parts] for t in range(sets)], refs[sets * parts :]
    j, gots, outs, turned = pl.program_id(0), refs[:given], refs[given:-1], refs[-1]

    @pl.when(j == 0)
    def _():
        at = 0
        for src in srcs:
            turned[:, at : at + src.shape[0]] = src[...].T
            at += src.shape[0]

    for t in range(sets):

        @pl.when((j >= t * exp_dev) & (j < (t + 1) * exp_dev))
        def _():
            rhs = jnp.concatenate([ref[...] for ref in rhss[t]], 0)
            total = jnp.dot(turned[...], rhs, preferred_element_type=jnp.float32)
            if not gots:
                if len(outs) == 1:
                    outs[0][...] = total.astype(jnp.bfloat16)
                for n, out in enumerate(outs if len(outs) > 1 else []):

                    @pl.when(j == n)
                    def _():
                        out[...] = total.astype(jnp.bfloat16)

                return
            for e in range(exp_dev):

                @pl.when(j == t * exp_dev + e)
                def _():
                    outs[t][:, e, :] = total + gots[e % given][...].astype(jnp.float32)


def grad_pass(srcs, sets, block, own, exp_dev, name, got=(), apart=False):
    rows, hid = sum(src.shape[0] for src in srcs), sets[0][0].shape[1] // exp_dev
    cols = len(sets) * exp_dev * hid
    in_specs = [pl.BlockSpec((src.shape[0], own), lambda j, b: (0, b[0])) for src in srcs]
    for t, rhss in enumerate(sets):
        in_specs += [
            pl.BlockSpec(
                (rhs.shape[0], hid),
                functools.partial(
                    lambda first, j, b: (0, jnp.clip(j - first, 0, exp_dev - 1)), t * exp_dev
                ),
            )
            for rhs in rhss
        ]
    out_specs = [pl.BlockSpec((own, hid), lambda j, b: (0, j))]
    out_shape = [jax.ShapeDtypeStruct((own, cols), jnp.bfloat16)]
    operands = [*srcs, *(rhs for rhss in sets for rhs in rhss)]
    if apart:
        out_specs = [pl.BlockSpec((own, hid), lambda j, b: (0, 0))] * (cols // hid)
        out_shape = [jax.ShapeDtypeStruct((own, hid), jnp.bfloat16)] * (cols // hid)
    if got:
        apart_spec = pl.BlockSpec((own, hid), lambda j, b: (0, 0))
        in_specs += out_specs if len(got) == 1 else [apart_spec] * len(got)
        operands += got
        out_specs = [pl.BlockSpec((own, exp_dev, hid), lambda j, b: (0, 0, 0))] * len(sets)
        out_shape = [jax.ShapeDtypeStruct((own, exp_dev, hid), jnp.float32)] * len(sets)
    return pl.pallas_call(
        functools.partial(grad_kernel, len(srcs), len(sets), len(sets[0]), exp_dev, len(got)),
        grid_spec=pltpu.PrefetchScalarGridSpec(
            num_scalar_prefetch=1,
            grid=(len(sets) * exp_dev,),
            in_specs=in_specs,
            out_specs=out_specs,
            scratch_shapes=[pltpu.VMEM((own, rows), jnp.bfloat16)],
        ),
        out_shape=out_shape,
        compiler_params=pltpu.CompilerParams(vmem_limit_bytes=GRAD_BYTES),
        cost_estimate=pl.CostEstimate(
            flops=2 * rows * own * cols // DECLARED,
            bytes_accessed=2 * (rows * (own + cols) + own * cols) // DECLARED,
            transcendentals=0,
        ),
        name=name,
    )(block, *operands)


def sum_kernel(keep_ref, *refs):
    gots, out_ref = refs[:-1], refs[-1]
    hid = out_ref.shape[2]
    for e, got_ref in enumerate(gots):
        keep = keep_ref[:, e * hid : (e + 1) * hid].astype(jnp.float32)
        out_ref[:, e, :] = keep + got_ref[...].astype(jnp.float32)


def sum_pass(keep, gots):
    rows, cols = keep.shape
    tile, hid = min(128, rows), cols // len(gots)
    return pl.pallas_call(
        sum_kernel,
        grid=(rows // tile,),
        in_specs=[pl.BlockSpec((tile, cols), lambda i: (i, 0))]
        + [pl.BlockSpec((tile, hid), lambda i: (i, 0))] * len(gots),
        out_specs=pl.BlockSpec((tile, len(gots), hid), lambda i: (i, 0, 0)),
        out_shape=jax.ShapeDtypeStruct((rows, len(gots), hid), jnp.float32),
        compiler_params=pltpu.CompilerParams(vmem_limit_bytes=SUM_BYTES),
        name="sum_pass",
    )(keep, *gots)


def dense_form(tokens, routes, route_weights, cotangent, gate_proj, up_proj, down_proj):
    tok_dev, width = tokens.shape
    exp_dev, hid = down_proj.shape[:2]
    cols = exp_dev * hid
    n_dp = lax.axis_size("dp")
    own = width // n_dp
    experts = exp_dev * lax.axis_size("expert")
    mine = (lax.axis_index("expert") * exp_dev).reshape(1).astype(jnp.int32)
    here = lax.axis_index("dp")

    named = routes[:, :, None] == jnp.arange(experts, dtype=jnp.int32)[None, None, :]
    dense = jnp.sum(jnp.where(named, route_weights[:, :, None], 0.0), axis=1)
    high = lax.reduce_precision(dense, 8, 7)
    space = -(2 * experts) % 128
    xc = jnp.concatenate(
        [tokens, cotangent, high.astype(jnp.bfloat16), (dense - high).astype(jnp.bfloat16)]
        + [jnp.zeros((tok_dev, space), jnp.bfloat16)],
        1,
    )
    wgu = jnp.concatenate(
        [gate_proj[e] for e in range(exp_dev)] + [up_proj[e] for e in range(exp_dev)], 1
    )
    wd = down_proj.reshape(cols, width)

    def work(groups, with_rwg, **kwargs):
        return list(routes_pass(groups, mine, wgu, wd, hid, experts, with_rwg, **kwargs))

    def across(*blocks):
        return [swap(block, "expert", 1) for block in blocks]

    half = tok_dev // 2
    by_x, by_y = 2, 4
    mate = swap(xc, "dp", 2)
    near_x, near_y = together([swap(xc, "expert", by_x), swap(xc, "expert", by_y)])
    near = [xc, near_x, near_y]
    own_far, far_near_x, far_near_y = across(*near)
    first = [xc, near_x, own_far, far_near_x]
    corner = [swap(near_x[:half], "expert", by_y), swap(near_y[half:], "expert", by_x)]
    made = work([first[:2], first[2:]], True)
    corner_x, corner_y, mate, *first_made = together([*corner, mate, *made])
    corner = [corner_x, corner_y]
    second = [near_y, *corner, far_near_y, *across(*corner), mate, *across(mate)]
    made = work([second[:3], second[3:6], second[6:]], True)
    far_x, far_y, *second_made = together(
        [swap(mate, "expert", by_x), swap(mate, "expert", by_y), *made]
    )
    third, passed = [far_x, far_y], across(far_x, far_y)
    corner = [swap(far_x[:half], "expert", by_y), swap(far_y[half:], "expert", by_x)]
    made = work([third], False)
    corner_x, corner_y, *third_made = together([*corner, *made])
    fourth = [*passed, corner_x, corner_y, *across(corner_x, corner_y)]
    fourth_made = work([fourth[:2], fourth[2:]], False)
    arrived = first + second + third + fourth
    units = [first_made, second_made, third_made, fourth_made]
    hws, dgs, dus = [[values[n] for values in units] for n in range(3)]
    mates, token = (here ^ 1).reshape(1).astype(jnp.int32), here.reshape(1).astype(jnp.int32)

    def grad(sets, block, of_cot, name, got=(), apart=False):
        block = block + (n_dp if of_cot else 0)
        return grad_pass(arrived, sets, block, own, exp_dev, name, got, apart)

    gate_send, mates = together([*grad([dgs], mates, False, "gate_send"), mates])
    *up_send, after = together([*grad([dus], mates, False, "up_send", apart=True), mates])
    shares = out_pass([(first_made, 4 * tok_dev), (second_made, 4 * tok_dev)], wgu, wd, after)
    *shares, mates = together([*shares, after])
    down_send = grad([hws], mates, True, "down_send", apart=True)
    *values, up_last, gate_got, token = together(
        [*shares, *down_send, *(swap(send, "dp", 1) for send in up_send[:-1])]
        + [up_send[-1], swap(gate_send, "dp", 1), token]
    )
    shares, down_send, up_got = values[:4], values[4 : 4 + exp_dev], values[4 + exp_dev :]
    last = add_to(shares[2], *across(shares[3]))
    chip = add_to(shares[0], *across(shares[1]))
    last, token = together([last, token])
    of_y, corner = last[:tok_dev], last[tok_dev:]
    (down_keep,) = grad([hws], token, True, "down_keep")
    to_x, to_y, up_last, chip, down_keep, token, *down_send = together(
        [
            swap(corner[:half], "expert", by_y),
            swap(corner[half:], "expert", by_x),
            swap(up_last, "dp", 1),
            chip,
            down_keep,
            token,
            *down_send,
        ]
    )
    *down_got, last_got = [swap(send, "dp", 1) for send in down_send]
    mine_too, of_x = chip[:tok_dev], chip[tok_dev:]
    of_x = join([add_to(of_x[:half], to_x), of_x[half:]])
    of_y = join([of_y[:half], add_to(of_y[half:], to_y)])
    (gate_grad,) = grad([dgs], token, False, "gate_grad", got=[gate_got])
    (up_grad,) = grad([dus], token, False, "up_grad", got=[*up_got, up_last])
    from_x, from_y, gate_grad, up_grad, *down_got = together(
        [swap(of_x, "expert", by_x), swap(of_y, "expert", by_y), gate_grad, up_grad, *down_got]
    )
    summed = sum(v.astype(jnp.float32) for v in (mine_too, from_x, from_y))
    tail = summed[:, 2 * width :]
    rwg_dense = tail[:, :experts] + tail[:, experts : 2 * experts]
    route_weight_grad = jnp.sum(jnp.where(named, rwg_dense[:, None, :], 0.0), axis=2)
    summed = summed[:, : 2 * width].astype(jnp.bfloat16)
    layer_output, input_grad, route_weight_grad, last_got = together(
        [summed[:, :width], summed[:, width:], route_weight_grad, last_got]
    )
    grads = [gate_grad, up_grad, sum_pass(down_keep, [*down_got, last_got])]
    return (layer_output, input_grad, route_weight_grad, *grads)


def swish_parts(gate_pre):
    sig_value = jax.nn.sigmoid(gate_pre)
    return (gate_pre * sig_value, sig_value * (1.0 + gate_pre * (1.0 - sig_value)))


def project_in(arrived, gate_proj, up_proj):
    gate_pre = jnp.einsum("secd,edh->sech", arrived, gate_proj, preferred_element_type=jnp.float32)
    up_pre = jnp.einsum("secd,edh->sech", arrived, up_proj, preferred_element_type=jnp.float32)
    return (gate_pre, up_pre)


def project_out(gate_pre, up_pre, down_proj):
    swish = swish_parts(gate_pre)[0]
    hidden = (swish * up_pre).astype(jnp.bfloat16)
    return jnp.einsum(
        "sech,ehd->secd", hidden, down_proj, preferred_element_type=jnp.float32
    ).astype(jnp.bfloat16)


def three_terms(feat_rows, cot_rows, d_gate, d_up, hidden):
    return jnp.stack(
        [
            jnp.einsum("secd,sech->deh", feat_rows, d_gate, preferred_element_type=jnp.float32),
            jnp.einsum("secd,sech->deh", feat_rows, d_up, preferred_element_type=jnp.float32),
            jnp.einsum("secd,sech->deh", cot_rows, hidden, preferred_element_type=jnp.float32),
        ],
        axis=1,
    )


def slots_form(tokens, routes, route_weights, cotangent, gate_proj, up_proj, down_proj):
    tok_dev, model_width = tokens.shape
    top_count = routes.shape[1]
    exp_dev = gate_proj.shape[0]
    groups = lax.axis_size("expert")
    experts = exp_dev * groups
    capacity = 3 * tok_dev * top_count // (2 * experts)
    n_routes = tok_dev * top_count
    flat_expert = routes.reshape(-1)
    onehot = (flat_expert[:, None] == jnp.arange(experts, dtype=jnp.int32)[None, :]).astype(
        jnp.int32
    )
    before = jnp.cumsum(onehot, axis=0) - onehot
    position = jnp.sum(before * onehot, axis=1)
    slot_index = flat_expert * capacity + position
    slot_source = (
        jnp.full((experts * capacity,), n_routes, jnp.int32)
        .at[slot_index]
        .set(jnp.arange(n_routes, dtype=jnp.int32))
    )
    token_of = slot_source // top_count
    padded_x = jnp.concatenate([tokens, jnp.zeros((1, model_width), tokens.dtype)], 0)
    outgoing = padded_x[token_of].reshape(groups, exp_dev, capacity, model_width)
    arrived = lax.all_to_all(outgoing, "expert", split_axis=0, concat_axis=0, tiled=True)
    gate_pre, up_pre = project_in(arrived, gate_proj, up_proj)
    expert_out, arrived, gate_pre, up_pre = (
        project_out(gate_pre, up_pre, down_proj),
        arrived,
        gate_pre,
        up_pre,
    )
    returned = lax.all_to_all(expert_out, "expert", split_axis=0, concat_axis=0, tiled=True)
    route_out = returned.reshape(experts * capacity, model_width)[slot_index].reshape(
        tok_dev, top_count, model_width
    )
    layer_output = jnp.sum(
        route_out.astype(jnp.float32) * route_weights[:, :, None], axis=1
    ).astype(jnp.bfloat16)
    route_weight_grad = jnp.einsum(
        "tkd,td->tk", route_out, cotangent, preferred_element_type=jnp.float32
    )
    route_cot = (route_weights[:, :, None] * cotangent[:, None, :].astype(jnp.float32)).astype(
        jnp.bfloat16
    )
    padded_cot = jnp.concatenate(
        [route_cot.reshape(n_routes, model_width), jnp.zeros((1, model_width), jnp.bfloat16)], 0
    )
    cot_out = padded_cot[slot_source].reshape(groups, exp_dev, capacity, model_width)
    arrived_cot = lax.all_to_all(cot_out, "expert", split_axis=0, concat_axis=0, tiled=True)
    swish, d_swish = swish_parts(gate_pre)
    hidden = (swish * up_pre).astype(jnp.bfloat16)
    d_hidden = jnp.einsum(
        "secd,ehd->sech", arrived_cot, down_proj, preferred_element_type=jnp.float32
    )
    d_gate = (d_hidden * up_pre * d_swish).astype(jnp.bfloat16)
    d_up = (d_hidden * swish).astype(jnp.bfloat16)
    route_dx = (
        jnp.einsum("sech,edh->secd", d_gate, gate_proj, preferred_element_type=jnp.float32)
        + jnp.einsum("sech,edh->secd", d_up, up_proj, preferred_element_type=jnp.float32)
    ).astype(jnp.bfloat16)
    dx_back = lax.all_to_all(route_dx, "expert", split_axis=0, concat_axis=0, tiled=True)
    token_dx = dx_back.reshape(experts * capacity, model_width)[slot_index].reshape(
        tok_dev, top_count, model_width
    )
    input_grad = jnp.sum(token_dx.astype(jnp.float32), axis=1).astype(jnp.bfloat16)
    full_terms = three_terms(arrived, arrived_cot, d_gate, d_up, hidden)
    shares = lax.psum_scatter(
        full_terms.astype(jnp.bfloat16), "dp", scatter_dimension=0, tiled=True
    ).astype(jnp.float32)
    return (layer_output, input_grad, route_weight_grad, shares[:, 0], shares[:, 1], shares[:, 2])


def on_device(tokens, routes, route_weights, cotangent, gate_proj, up_proj, down_proj):
    groups = lax.axis_size("expert")
    few = gate_proj.shape[0] * groups <= 2 * routes.shape[1]
    square = groups == 2 * 2 * 2 and lax.axis_size("dp") == 2 * 2
    form = dense_form if few and square else slots_form
    return form(tokens, routes, route_weights, cotangent, gate_proj, up_proj, down_proj)


def solution(mesh):
    rows = P(("dp", "expert"), None)
    held = P("expert", None, None)
    owned = P("dp", "expert", None)
    return jax.shard_map(
        on_device,
        mesh=mesh,
        in_specs=(rows, rows, rows, rows, held, held, held),
        out_specs=(rows, rows, rows, owned, owned, owned),
        check_vma=False,
    )
```

```python
import functools

import jax
import jax.numpy as jnp
from jax import lax
from jax.experimental import pallas as pl
from jax.experimental.pallas import tpu as pltpu
from jax.sharding import PartitionSpec as P

MIB = 1024 * 1024
DECLARED = 1 << 20
ROUTES_BYTES, OUT_BYTES, GRAD_BYTES, SUM_BYTES = 56 * MIB, 56 * MIB, 56 * MIB, 8 * MIB


def swap(value, axis, mask):
    return lax.ppermute(value, axis, [(i, i ^ mask) for i in range(lax.axis_size(axis))])


def together(values):
    return list(lax.optimization_barrier(tuple(values)))


def join(parts):
    return parts[0] if len(parts) == 1 else jnp.concatenate(parts, 0)


def add_to(kept, received):
    return (kept.astype(jnp.float32) + received.astype(jnp.float32)).astype(kept.dtype)


def tile_of(cols):
    return 256 if cols % 256 == 0 else 128


def split_in_two(value):
    high = value.astype(jnp.bfloat16)
    return high, (value - high.astype(jnp.float32)).astype(jnp.bfloat16)


def by_expert(values, lane, hid):
    spread = values[-1]
    for e in range(len(values) - 2, -1, -1):
        spread = jnp.where(lane < (e + 1) * hid, values[e], spread)
    return spread


def routes_kernel(counts, hid, experts, with_rwg, mine_ref, *refs):
    xcs, (wg, wu, wd, hw, dg, du, *more) = refs[: sum(counts)], refs[sum(counts) :]
    extra_ref, sums = more[0] if with_rwg else None, more[-1]
    j, (tile, width) = pl.program_id(0), wd.shape
    held = sums.shape[1]

    @pl.when(j == 0)
    def _():
        sums[...] = jnp.zeros(sums.shape, jnp.float32)

    mine = mine_ref[0]
    end = 0
    for count in counts:
        group, xcs = xcs[:count], xcs[count:]
        x = jnp.concatenate([ref[:, :width] for ref in group], 0)
        c = jnp.concatenate([ref[:, width : 2 * width] for ref in group], 0)
        tail = jnp.concatenate([ref[:, 2 * width :] for ref in group], 0).astype(jnp.float32)
        rows = slice(end, end + x.shape[0])
        end = rows.stop
        lane = lax.broadcasted_iota(jnp.int32, (x.shape[0], tile), 1) + j * tile
        spot = lax.broadcasted_iota(jnp.int32, tail.shape, 1)
        spots = [(spot == mine + e, spot == experts + mine + e) for e in range(held)]
        weights = [
            jnp.sum(jnp.where(high | low, tail, 0.0), axis=1, keepdims=True) for high, low in spots
        ]
        gate = jnp.dot(x, wg[...], preferred_element_type=jnp.float32)
        up = jnp.dot(x, wu[...], preferred_element_type=jnp.float32)
        d_plain = lax.dot_general(
            c,
            wd[...],
            (((1,), (1,)), ((), ())),
            preferred_element_type=jnp.float32,
        )
        weight = by_expert(weights, lane, hid)
        sig = jax.nn.sigmoid(gate)
        swish = gate * sig
        hidden = swish * up
        d_hidden = d_plain * weight
        hw[rows, :] = (hidden * weight).astype(jnp.bfloat16)
        dg[rows, :] = (d_hidden * up * (sig * (1.0 + gate * (1.0 - sig)))).astype(jnp.bfloat16)
        du[rows, :] = (d_hidden * swish).astype(jnp.bfloat16)
        if not with_rwg:
            continue
        product = hidden * d_plain
        for e in range(held):
            inside = (lane >= e * hid) & (lane < (e + 1) * hid)
            sums[rows, e : e + 1] += jnp.sum(
                jnp.where(inside, product, 0.0), axis=1, keepdims=True
            )

    if with_rwg:

        @pl.when(j == pl.num_programs(0) - 1)
        def _():
            spot = lax.broadcasted_iota(jnp.int32, extra_ref.shape, 1)
            placed = jnp.zeros(extra_ref.shape, jnp.float32)
            for e in range(held):
                top, rest = split_in_two(sums[:, e : e + 1])
                placed = jnp.where(spot == mine + e, top.astype(jnp.float32), placed)
                placed = jnp.where(spot == experts + mine + e, rest.astype(jnp.float32), placed)
            extra_ref[...] = placed.astype(jnp.bfloat16)


def routes_pass(groups, mine, wgu, wd, hid, experts, with_rwg, declared=DECLARED):
    counts, blocks = [len(group) for group in groups], [b for group in groups for b in group]
    rows, wide = sum(block.shape[0] for block in blocks), blocks[0].shape[1]
    cols, width = wd.shape
    tile, once = tile_of(cols), pl.Buffered(1)
    steps = cols // tile
    extra = wide - 2 * width
    return pl.pallas_call(
        functools.partial(routes_kernel, counts, hid, experts, with_rwg),
        grid=(steps,),
        in_specs=[pl.BlockSpec(memory_space=pltpu.SMEM)]
        + [pl.BlockSpec(b.shape, lambda j: (0, 0), pipeline_mode=once) for b in blocks]
        + [
            pl.BlockSpec((width, tile), lambda j: (0, j)),
            pl.BlockSpec((width, tile), lambda j: (0, steps + j)),
            pl.BlockSpec((tile, width), lambda j: (j, 0)),
        ],
        out_specs=[pl.BlockSpec((rows, tile), lambda j: (0, j))] * 3
        + [pl.BlockSpec((rows, extra), lambda j: (0, 0))] * with_rwg,
        out_shape=[jax.ShapeDtypeStruct((rows, cols), jnp.bfloat16)] * 3
        + [jax.ShapeDtypeStruct((rows, extra), jnp.bfloat16)] * with_rwg,
        scratch_shapes=[pltpu.VMEM((rows, cols // hid), jnp.float32)],
        compiler_params=pltpu.CompilerParams(vmem_limit_bytes=ROUTES_BYTES),
        cost_estimate=pl.CostEstimate(
            flops=6 * rows * width * cols // declared,
            bytes_accessed=2 * (2 * rows * width + 3 * width * cols) // declared,
            transcendentals=0,
        ),
        name="routes_pass",
    )(mine, *blocks, wgu, wgu, wd)


def out_kernel(sections, token_ref, *refs):
    made, (wd, wgu), outs = refs[: 4 * sections], refs[4 * sections : 4 * sections + 2], refs[4 * sections + 2 :]
    j, steps = pl.program_id(0), (pl.num_programs(0) - 1) // 2
    cols = wd.shape[0]

    def put(p, value):
        half, tile = value.shape[0] // 2, value.shape[1]
        outs[2 * p][:, :tile] = value[:half].astype(jnp.bfloat16)
        outs[2 * p + 1][:, :tile] = value[half:].astype(jnp.bfloat16)

    for p in range(sections):
        hw, dg, du, extra = made[4 * p : 4 * p + 4]

        @pl.when(j < steps)
        def _():
            put(p, jnp.dot(hw[...], wd[...], preferred_element_type=jnp.float32))

        @pl.when((j >= steps) & (j < 2 * steps))
        def _():
            put(
                p,
                sum(
                    lax.dot_general(
                        d[...],
                        wgu[:, at : at + cols],
                        (((1,), (1,)), ((), ())),
                        preferred_element_type=jnp.float32,
                    )
                    for d, at in ((dg, 0), (du, cols))
                ),
            )

        @pl.when(j == 2 * steps)
        def _():
            put(p, extra[...])


def out_pass(sections, wgu, wd, token):
    cols, width = wd.shape
    tile = 512 if width % 512 == 0 else 128
    steps, wide = width // tile, 2 * width + sections[0][0][3].shape[1]
    flat, specs, outs = [], [], []
    for values, rows in sections:
        flat += values
        specs += [
            pl.BlockSpec((rows, v.shape[1]), lambda j: (0, 0), pipeline_mode=pl.Buffered(1))
            for v in values
        ]
        outs += [jax.ShapeDtypeStruct((rows // 2, wide), jnp.bfloat16)] * 2
    total = sum(rows for _, rows in sections)
    got = pl.pallas_call(
        functools.partial(out_kernel, len(sections)),
        grid=(2 * steps + 1,),
        in_specs=[pl.BlockSpec(memory_space=pltpu.SMEM)]
        + specs
        + [
            pl.BlockSpec((cols, tile), lambda j: (0, jnp.minimum(j, steps - 1))),
            pl.BlockSpec((tile, 2 * cols), lambda j: (jnp.clip(j - steps, 0, steps - 1), 0)),
        ],
        out_specs=[pl.BlockSpec((o.shape[0], tile), lambda j: (0, j)) for o in outs],
        out_shape=outs,
        compiler_params=pltpu.CompilerParams(vmem_limit_bytes=OUT_BYTES),
        cost_estimate=pl.CostEstimate(
            flops=6 * total * width * cols // DECLARED,
            bytes_accessed=2 * (2 * total * width + 3 * width * cols) // DECLARED,
            transcendentals=0,
        ),
        name="out_pass",
    )(token, *flat, wd, wgu)
    return list(got)


def grad_kernel(sources, sets, parts, exp_dev, given, block_ref, *refs):
    srcs, refs = refs[:sources], refs[sources:]
    rhss, refs = [refs[t * parts : (t + 1) * parts] for t in range(sets)], refs[sets * parts :]
    j, gots, outs, turned = pl.program_id(0), refs[:given], refs[given:-1], refs[-1]

    @pl.when(j == 0)
    def _():
        at = 0
        for src in srcs:
            turned[:, at : at + src.shape[0]] = src[...].T
            at += src.shape[0]

    for t in range(sets):

        @pl.when((j >= t * exp_dev) & (j < (t + 1) * exp_dev))
        def _():
            rhs = jnp.concatenate([ref[...] for ref in rhss[t]], 0)
            total = jnp.dot(turned[...], rhs, preferred_element_type=jnp.float32)
            if not gots:
                if len(outs) == 1:
                    outs[0][...] = total.astype(jnp.bfloat16)
                for n, out in enumerate(outs if len(outs) > 1 else []):

                    @pl.when(j == n)
                    def _():
                        out[...] = total.astype(jnp.bfloat16)

                return
            for e in range(exp_dev):

                @pl.when(j == t * exp_dev + e)
                def _():
                    outs[t][:, e, :] = total + gots[e % given][...].astype(jnp.float32)


def grad_pass(srcs, sets, block, own, exp_dev, name, got=(), apart=False):
    rows, hid = sum(src.shape[0] for src in srcs), sets[0][0].shape[1] // exp_dev
    cols = len(sets) * exp_dev * hid
    in_specs = [pl.BlockSpec((src.shape[0], own), lambda j, b: (0, b[0])) for src in srcs]
    for t, rhss in enumerate(sets):
        in_specs += [
            pl.BlockSpec(
                (rhs.shape[0], hid),
                functools.partial(
                    lambda first, j, b: (0, jnp.clip(j - first, 0, exp_dev - 1)), t * exp_dev
                ),
            )
            for rhs in rhss
        ]
    out_specs = [pl.BlockSpec((own, hid), lambda j, b: (0, j))]
    out_shape = [jax.ShapeDtypeStruct((own, cols), jnp.bfloat16)]
    operands = [*srcs, *(rhs for rhss in sets for rhs in rhss)]
    if apart:
        out_specs = [pl.BlockSpec((own, hid), lambda j, b: (0, 0))] * (cols // hid)
        out_shape = [jax.ShapeDtypeStruct((own, hid), jnp.bfloat16)] * (cols // hid)
    if got:
        apart_spec = pl.BlockSpec((own, hid), lambda j, b: (0, 0))
        in_specs += out_specs if len(got) == 1 else [apart_spec] * len(got)
        operands += got
        out_specs = [pl.BlockSpec((own, exp_dev, hid), lambda j, b: (0, 0, 0))] * len(sets)
        out_shape = [jax.ShapeDtypeStruct((own, exp_dev, hid), jnp.float32)] * len(sets)
    return pl.pallas_call(
        functools.partial(grad_kernel, len(srcs), len(sets), len(sets[0]), exp_dev, len(got)),
        grid_spec=pltpu.PrefetchScalarGridSpec(
            num_scalar_prefetch=1,
            grid=(len(sets) * exp_dev,),
            in_specs=in_specs,
            out_specs=out_specs,
            scratch_shapes=[pltpu.VMEM((own, rows), jnp.bfloat16)],
        ),
        out_shape=out_shape,
        compiler_params=pltpu.CompilerParams(vmem_limit_bytes=GRAD_BYTES),
        cost_estimate=pl.CostEstimate(
            flops=2 * rows * own * cols // DECLARED,
            bytes_accessed=2 * (rows * (own + cols) + own * cols) // DECLARED,
            transcendentals=0,
        ),
        name=name,
    )(block, *operands)


def sum_kernel(keep_ref, *refs):
    gots, out_ref = refs[:-1], refs[-1]
    hid = out_ref.shape[2]
    for e, got_ref in enumerate(gots):
        keep = keep_ref[:, e * hid : (e + 1) * hid].astype(jnp.float32)
        out_ref[:, e, :] = keep + got_ref[...].astype(jnp.float32)


def sum_pass(keep, gots):
    rows, cols = keep.shape
    tile, hid = min(256, rows), cols // len(gots)
    return pl.pallas_call(
        sum_kernel,
        grid=(rows // tile,),
        in_specs=[pl.BlockSpec((tile, cols), lambda i: (i, 0))]
        + [pl.BlockSpec((tile, hid), lambda i: (i, 0))] * len(gots),
        out_specs=pl.BlockSpec((tile, len(gots), hid), lambda i: (i, 0, 0)),
        out_shape=jax.ShapeDtypeStruct((rows, len(gots), hid), jnp.float32),
        compiler_params=pltpu.CompilerParams(vmem_limit_bytes=SUM_BYTES),
        name="sum_pass",
    )(keep, *gots)


def dense_form(tokens, routes, route_weights, cotangent, gate_proj, up_proj, down_proj):
    tok_dev, width = tokens.shape
    exp_dev, hid = down_proj.shape[:2]
    cols = exp_dev * hid
    n_dp = lax.axis_size("dp")
    own = width // n_dp
    experts = exp_dev * lax.axis_size("expert")
    mine = (lax.axis_index("expert") * exp_dev).reshape(1).astype(jnp.int32)
    here = lax.axis_index("dp")

    named = routes[:, :, None] == jnp.arange(experts, dtype=jnp.int32)[None, None, :]
    dense = jnp.sum(jnp.where(named, route_weights[:, :, None], 0.0), axis=1)
    high = lax.reduce_precision(dense, 8, 7)
    space = -(2 * experts) % 128
    xc = jnp.concatenate(
        [tokens, cotangent, high.astype(jnp.bfloat16), (dense - high).astype(jnp.bfloat16)]
        + [jnp.zeros((tok_dev, space), jnp.bfloat16)],
        1,
    )
    wgu = jnp.concatenate(
        [gate_proj[e] for e in range(exp_dev)] + [up_proj[e] for e in range(exp_dev)], 1
    )
    wd = down_proj.reshape(cols, width)

    def work(groups, with_rwg, **kwargs):
        return list(routes_pass(groups, mine, wgu, wd, hid, experts, with_rwg, **kwargs))

    def across(*blocks):
        return [swap(block, "expert", 1) for block in blocks]

    half = tok_dev // 2
    by_x, by_y = 2, 4
    mate = swap(xc, "dp", 2)
    near_x, near_y = together([swap(xc, "expert", by_x), swap(xc, "expert", by_y)])
    near = [xc, near_x, near_y]
    own_far, far_near_x, far_near_y = across(*near)
    first = [xc, near_x, own_far, far_near_x]
    corner = [swap(near_x[:half], "expert", by_y), swap(near_y[half:], "expert", by_x)]
    made = work([first[:2], first[2:]], True)
    corner_x, corner_y, mate, *first_made = together([*corner, mate, *made])
    corner = [corner_x, corner_y]
    second = [near_y, *corner, far_near_y, *across(*corner), mate, *across(mate)]
    made = work([second[:3], second[3:6], second[6:]], True)
    far_x, far_y, *second_made = together(
        [swap(mate, "expert", by_x), swap(mate, "expert", by_y), *made]
    )
    third, passed = [far_x, far_y], across(far_x, far_y)
    corner = [swap(far_x[:half], "expert", by_y), swap(far_y[half:], "expert", by_x)]
    made = work([third], False)
    corner_x, corner_y, *third_made = together([*corner, *made])
    fourth = [*passed, corner_x, corner_y, *across(corner_x, corner_y)]
    fourth_made = work([fourth[:2], fourth[2:]], False)
    arrived = first + second + third + fourth
    units = [first_made, second_made, third_made, fourth_made]
    hws, dgs, dus = [[values[n] for values in units] for n in range(3)]
    mates, token = (here ^ 1).reshape(1).astype(jnp.int32), here.reshape(1).astype(jnp.int32)

    def grad(sets, block, of_cot, name, got=(), apart=False):
        block = block + (n_dp if of_cot else 0)
        return grad_pass(arrived, sets, block, own, exp_dev, name, got, apart)

    gate_send, mates = together([*grad([dgs], mates, False, "gate_send"), mates])
    *up_send, after = together([*grad([dus], mates, False, "up_send", apart=True), mates])
    shares = out_pass([(first_made, 4 * tok_dev), (second_made, 4 * tok_dev)], wgu, wd, after)
    *shares, mates = together([*shares, after])
    down_send = grad([hws], mates, True, "down_send", apart=True)
    *values, up_last, gate_got, token = together(
        [*shares, *down_send, *(swap(send, "dp", 1) for send in up_send[:-1])]
        + [up_send[-1], swap(gate_send, "dp", 1), token]
    )
    shares, down_send, up_got = values[:4], values[4 : 4 + exp_dev], values[4 + exp_dev :]
    last = add_to(shares[2], *across(shares[3]))
    chip = add_to(shares[0], *across(shares[1]))
    last, token = together([last, token])
    of_y, corner = last[:tok_dev], last[tok_dev:]
    (down_keep,) = grad([hws], token, True, "down_keep")
    to_x, to_y, up_last, chip, down_keep, token, *down_send = together(
        [
            swap(corner[:half], "expert", by_y),
            swap(corner[half:], "expert", by_x),
            swap(up_last, "dp", 1),
            chip,
            down_keep,
            token,
            *down_send,
        ]
    )
    *down_got, last_got = [swap(send, "dp", 1) for send in down_send]
    mine_too, of_x = chip[:tok_dev], chip[tok_dev:]
    of_x = join([add_to(of_x[:half], to_x), of_x[half:]])
    of_y = join([of_y[:half], add_to(of_y[half:], to_y)])
    (gate_grad,) = grad([dgs], token, False, "gate_grad", got=[gate_got])
    (up_grad,) = grad([dus], token, False, "up_grad", got=[*up_got, up_last])
    from_x, from_y, gate_grad, up_grad, *down_got = together(
        [swap(of_x, "expert", by_x), swap(of_y, "expert", by_y), gate_grad, up_grad, *down_got]
    )
    summed = sum(v.astype(jnp.float32) for v in (mine_too, from_x, from_y))
    tail = summed[:, 2 * width :]
    rwg_dense = tail[:, :experts] + tail[:, experts : 2 * experts]
    route_weight_grad = jnp.sum(jnp.where(named, rwg_dense[:, None, :], 0.0), axis=2)
    summed = summed[:, : 2 * width].astype(jnp.bfloat16)
    layer_output, input_grad, route_weight_grad, last_got = together(
        [summed[:, :width], summed[:, width:], route_weight_grad, last_got]
    )
    grads = [gate_grad, up_grad, sum_pass(down_keep, [*down_got, last_got])]
    return (layer_output, input_grad, route_weight_grad, *grads)


def swish_parts(gate_pre):
    sig_value = jax.nn.sigmoid(gate_pre)
    return (gate_pre * sig_value, sig_value * (1.0 + gate_pre * (1.0 - sig_value)))


def project_in(arrived, gate_proj, up_proj):
    gate_pre = jnp.einsum("secd,edh->sech", arrived, gate_proj, preferred_element_type=jnp.float32)
    up_pre = jnp.einsum("secd,edh->sech", arrived, up_proj, preferred_element_type=jnp.float32)
    return (gate_pre, up_pre)


def project_out(gate_pre, up_pre, down_proj):
    swish = swish_parts(gate_pre)[0]
    hidden = (swish * up_pre).astype(jnp.bfloat16)
    return jnp.einsum(
        "sech,ehd->secd", hidden, down_proj, preferred_element_type=jnp.float32
    ).astype(jnp.bfloat16)


def three_terms(feat_rows, cot_rows, d_gate, d_up, hidden):
    return jnp.stack(
        [
            jnp.einsum("secd,sech->deh", feat_rows, d_gate, preferred_element_type=jnp.float32),
            jnp.einsum("secd,sech->deh", feat_rows, d_up, preferred_element_type=jnp.float32),
            jnp.einsum("secd,sech->deh", cot_rows, hidden, preferred_element_type=jnp.float32),
        ],
        axis=1,
    )


def slots_form(tokens, routes, route_weights, cotangent, gate_proj, up_proj, down_proj):
    tok_dev, model_width = tokens.shape
    top_count = routes.shape[1]
    exp_dev = gate_proj.shape[0]
    groups = lax.axis_size("expert")
    experts = exp_dev * groups
    capacity = 3 * tok_dev * top_count // (2 * experts)
    n_routes = tok_dev * top_count
    flat_expert = routes.reshape(-1)
    onehot = (flat_expert[:, None] == jnp.arange(experts, dtype=jnp.int32)[None, :]).astype(
        jnp.int32
    )
    before = jnp.cumsum(onehot, axis=0) - onehot
    position = jnp.sum(before * onehot, axis=1)
    slot_index = flat_expert * capacity + position
    slot_source = (
        jnp.full((experts * capacity,), n_routes, jnp.int32)
        .at[slot_index]
        .set(jnp.arange(n_routes, dtype=jnp.int32))
    )
    token_of = slot_source // top_count
    padded_x = jnp.concatenate([tokens, jnp.zeros((1, model_width), tokens.dtype)], 0)
    outgoing = padded_x[token_of].reshape(groups, exp_dev, capacity, model_width)
    arrived = lax.all_to_all(outgoing, "expert", split_axis=0, concat_axis=0, tiled=True)
    gate_pre, up_pre = project_in(arrived, gate_proj, up_proj)
    expert_out, arrived, gate_pre, up_pre = (
        project_out(gate_pre, up_pre, down_proj),
        arrived,
        gate_pre,
        up_pre,
    )
    returned = lax.all_to_all(expert_out, "expert", split_axis=0, concat_axis=0, tiled=True)
    route_out = returned.reshape(experts * capacity, model_width)[slot_index].reshape(
        tok_dev, top_count, model_width
    )
    layer_output = jnp.sum(
        route_out.astype(jnp.float32) * route_weights[:, :, None], axis=1
    ).astype(jnp.bfloat16)
    route_weight_grad = jnp.einsum(
        "tkd,td->tk", route_out, cotangent, preferred_element_type=jnp.float32
    )
    route_cot = (route_weights[:, :, None] * cotangent[:, None, :].astype(jnp.float32)).astype(
        jnp.bfloat16
    )
    padded_cot = jnp.concatenate(
        [route_cot.reshape(n_routes, model_width), jnp.zeros((1, model_width), jnp.bfloat16)], 0
    )
    cot_out = padded_cot[slot_source].reshape(groups, exp_dev, capacity, model_width)
    arrived_cot = lax.all_to_all(cot_out, "expert", split_axis=0, concat_axis=0, tiled=True)
    swish, d_swish = swish_parts(gate_pre)
    hidden = (swish * up_pre).astype(jnp.bfloat16)
    d_hidden = jnp.einsum(
        "secd,ehd->sech", arrived_cot, down_proj, preferred_element_type=jnp.float32
    )
    d_gate = (d_hidden * up_pre * d_swish).astype(jnp.bfloat16)
    d_up = (d_hidden * swish).astype(jnp.bfloat16)
    route_dx = (
        jnp.einsum("sech,edh->secd", d_gate, gate_proj, preferred_element_type=jnp.float32)
        + jnp.einsum("sech,edh->secd", d_up, up_proj, preferred_element_type=jnp.float32)
    ).astype(jnp.bfloat16)
    dx_back = lax.all_to_all(route_dx, "expert", split_axis=0, concat_axis=0, tiled=True)
    token_dx = dx_back.reshape(experts * capacity, model_width)[slot_index].reshape(
        tok_dev, top_count, model_width
    )
    input_grad = jnp.sum(token_dx.astype(jnp.float32), axis=1).astype(jnp.bfloat16)
    full_terms = three_terms(arrived, arrived_cot, d_gate, d_up, hidden)
    shares = lax.psum_scatter(
        full_terms.astype(jnp.bfloat16), "dp", scatter_dimension=0, tiled=True
    ).astype(jnp.float32)
    return (layer_output, input_grad, route_weight_grad, shares[:, 0], shares[:, 1], shares[:, 2])


def on_device(tokens, routes, route_weights, cotangent, gate_proj, up_proj, down_proj):
    groups = lax.axis_size("expert")
    few = gate_proj.shape[0] * groups <= 2 * routes.shape[1]
    square = groups == 2 * 2 * 2 and lax.axis_size("dp") == 2 * 2
    form = dense_form if few and square else slots_form
    return form(tokens, routes, route_weights, cotangent, gate_proj, up_proj, down_proj)


def solution(mesh):
    rows = P(("dp", "expert"), None)
    held = P("expert", None, None)
    owned = P("dp", "expert", None)
    return jax.shard_map(
        on_device,
        mesh=mesh,
        in_specs=(rows, rows, rows, rows, held, held, held),
        out_specs=(rows, rows, rows, owned, owned, owned),
        check_vma=False,
    )
```
